32 devices in a mesh: dp: 16 (over z, x, core), mp: 2 (over y).
Axes of the slice: x: 2, y: 2, z: 4, core: 2. Of those that a mesh axis runs over, the one named last changes fastest.
Arguments:
- tokens: bfloat16 [18464, 1024], P(('dp', 'mp')), may hold values from -6 to 6
- ln1_gain: bfloat16 [1024], P(('dp', 'mp')), may hold values from 0.099609375 to 1.8984375
- ln1_bias: bfloat16 [1024], P(('dp', 'mp')), may hold values from -3 to 3
- qkv_weight: bfloat16 [1024, 3, 1024], P('dp', None, 'mp'), may hold values from -1 to 1
- qv_bias: bfloat16 [2, 16, 64], P(None, 'mp', 'dp'), may hold values from -3 to 3
- proj_weight: bfloat16 [1024, 1024], P('mp', 'dp'), may hold values from -1 to 1
- proj_bias: bfloat16 [1024], P(('dp', 'mp')), may hold values from -3 to 3
- ln2_gain: bfloat16 [1024], P(('dp', 'mp')), may hold values from 0.099609375 to 1.8984375
- ln2_bias: bfloat16 [1024], P(('dp', 'mp')), may hold values from -3 to 3
- fc1_weight: bfloat16 [1024, 4096], P('dp', 'mp'), may hold values from -0.1875 to 0.1875
- fc1_bias: bfloat16 [64, 64], P('mp', 'dp'), may hold values from -3 to 3
- fc2_weight: bfloat16 [4096, 1024], P('mp', 'dp'), may hold values from -0.09375 to 0.09375
- fc2_bias: bfloat16 [1024], P(('dp', 'mp')), may hold values from -3 to 3
- cotangent: bfloat16 [18464, 1024], P(('dp', 'mp')), may hold values from -6 to 6
Outputs:
- output: bfloat16 [18464, 1024], P(('dp', 'mp'))
- grad_tokens: float32 [18464, 1024], P(('dp', 'mp'))
- grad_ln1_gain: float32 [1024], P(('dp', 'mp'))
- grad_ln1_bias: float32 [1024], P(('dp', 'mp'))
- grad_qkv_weight: float32 [1024, 3, 1024], P('dp', None, 'mp')
- grad_qv_bias: float32 [2, 16, 64], P(None, 'mp', 'dp')
- grad_proj_weight: float32 [1024, 1024], P('mp', 'dp')
- grad_proj_bias: float32 [1024], P(('dp', 'mp'))
- grad_ln2_gain: float32 [1024], P(('dp', 'mp'))
- grad_ln2_bias: float32 [1024], P(('dp', 'mp'))
- grad_fc1_weight: float32 [1024, 4096], P('dp', 'mp')
- grad_fc1_bias: float32 [64, 64], P('mp', 'dp')
- grad_fc2_weight: float32 [4096, 1024], P('mp', 'dp')
- grad_fc2_bias: float32 [1024], P(('dp', 'mp'))
The draws below stay inside these ranges and needn't reach their ends.
All inputs are finite; a program needn't handle non-finite values.
Results may differ from the reference program's by a relative error of at most 0.017.
Values may be sent and summed in bfloat16 or wider, within the bound.
No kernel may reach another device: no remote copies, remote signals or barrier semaphores. Data moves between devices by JAX's collectives and lax.ppermute only.
A program may use at most 192 MiB of HBM per device.

```python
import math
import jax
import jax.numpy as jnp
from jax import lax

D = 1024
HEADS = 16
HD = 64
FF = 4096
SEQ = 577
IMG_DEV = 2
TOKENS = 18464
N_DP = 16


def draw_qkv_weight(key, part):
    key = jax.random.fold_in(key, 3)
    base = jax.random.normal(key, (D, 3, D), jnp.float32) * D ** (-0.5)
    return jnp.clip(base, -1.0, 1.0).astype(jnp.bfloat16)


def raised(entries, own_key, source, target, parts, factor):
    owner, partner = [(jnp.arange(entries.shape[axis_at]) // (entries.shape[axis_at] // parts)).reshape([-1 if axis == axis_at else 1 for axis in range(entries.ndim)]) for axis_at in (source, target)]
    chosen = jax.random.permutation(own_key, parts)[partner]
    strong = (owner == chosen) | (owner == (partner + parts // 2) % parts)
    return jnp.where(strong, factor * entries, entries)


def shard_levels(own_key, extent, split, least, largest):
    level = 1.0
    for axis_at, blocks in split:
        steps = jax.random.uniform(jax.random.fold_in(jax.random.fold_in(own_key, 6), axis_at), (blocks,), jnp.float32, least / len(split), largest / len(split))
        level = level * jnp.repeat(jnp.exp(steps), extent[axis_at] // blocks).reshape((-1,) + (1,) * (len(extent) - 1 - axis_at))
    return level


def centred(rng, shape, width, reach, shards=(), dtype=jnp.bfloat16):
    result = width * jax.random.normal(rng, shape, jnp.float32)
    if shards:
        result = result * shard_levels(rng, shape, shards, -0.22, 0.18)
    return jnp.clip(result, -reach, reach).astype(dtype)


def heavy_noise(stream_key, extent, deviation, bound, split, heavy, held_as=jnp.bfloat16):
    drawn = deviation * jax.random.normal(stream_key, extent, jnp.float32)
    if split:
        drawn = drawn * shard_levels(stream_key, extent, split, -0.22, 0.18)
    return jnp.clip(raised(drawn, jax.random.fold_in(stream_key, 3), *heavy), -bound, bound).astype(held_as)


def setup_inputs(seed: int = 0) -> dict:
    seeds = jax.random.split(jax.random.key(seed), 15)
    tokens = heavy_noise(seeds[0], (TOKENS, D), 1.0, 6.0, ((0, 32),), (0, 1, 32, 2.75))
    ln1_gain = jnp.clip(1.0 + 0.18 * jax.random.normal(seeds[1], (D,), jnp.float32), 0.099609375, 1.8984375).astype(jnp.bfloat16)
    ln1_bias = centred(seeds[2], (D,), 0.5, 3.0, ((0, 32),))
    qkv_weight = draw_qkv_weight(jax.random.fold_in(seeds[14], 71), 0)
    qv_bias = centred(seeds[4], (2, HEADS, HD), 0.5, 3.0, ((1, 2), (2, 16)))
    proj_weight = centred(seeds[5], (D, D), (D // 24) ** -0.5, 1.0, ((0, 2), (1, 16)))
    proj_bias = centred(seeds[6], (D,), 0.5, 3.0, ((0, 32),))
    ln2_gain = jnp.clip(1.0 + 0.18 * jax.random.normal(seeds[7], (D,), jnp.float32), 0.099609375, 1.8984375).astype(jnp.bfloat16)
    ln2_bias = centred(seeds[8], (D,), 0.5, 3.0, ((0, 32),))
    fc1_weight = centred(seeds[9], (D, FF), D ** -0.5, 0.1875, ((0, 16), (1, 2)))
    fc1_bias = centred(seeds[10], (FF // HD, HD), 0.5, 3.0, ((0, 2), (1, 16)))
    fc2_weight = centred(seeds[11], (FF, D), FF ** -0.5, 0.09375, ((0, 2), (1, 16)))
    fc2_bias = centred(seeds[12], (D,), 0.5, 3.0, ((0, 32),))
    cotangent = heavy_noise(seeds[13], (TOKENS, D), 1.0, 6.0, ((0, 32),), (0, 1, 32, 2.75))
    return {"tokens": tokens, "ln1_gain": ln1_gain, "ln1_bias": ln1_bias, "qkv_weight": qkv_weight, "qv_bias": qv_bias, "proj_weight": proj_weight, "proj_bias": proj_bias, "ln2_gain": ln2_gain, "ln2_bias": ln2_bias, "fc1_weight": fc1_weight, "fc1_bias": fc1_bias, "fc2_weight": fc2_weight, "fc2_bias": fc2_bias, "cotangent": cotangent}


EPS = 1e-06
SCALE = 0.125
HIGH = lax.Precision.HIGHEST

@jax.custom_vjp
def low(v):
    return lax.optimization_barrier(v.astype(jnp.bfloat16)).astype(jnp.float32)

@jax.custom_vjp
def low_back(v):
    return v

def low_keep(v):
    return (low(v), None)

def low_pass(kept, grad):
    return (grad,)

def back_keep(v):
    return (v, None)

def back_low(kept, grad):
    return (low(grad),)
low.defvjp(low_keep, low_pass)
low_back.defvjp(back_keep, back_low)

def matmul_high(left, right):
    return jnp.dot(left, right, precision=HIGH)

def layer_norm(inputs, scale_vec, shift_vec):
    row_mean = lax.optimization_barrier(jnp.mean(inputs, axis=-1, keepdims=True))
    centered = inputs - row_mean
    variance = lax.optimization_barrier(jnp.mean(jnp.square(centered), axis=-1, keepdims=True))
    return centered * lax.rsqrt(variance + EPS) * scale_vec + shift_vec

def gelu_exact(values):
    return 0.5 * values * (1.0 + lax.erf(values * (1.0 / math.sqrt(2.0))))

def attend_image(queries, key_heads, value_heads):
    raw = low_back(jnp.einsum('qhe,khe->hqk', queries, key_heads, precision=HIGH))
    scores = raw * SCALE
    row_max = lax.optimization_barrier(jnp.max(scores, axis=-1, keepdims=True))
    shifted = jnp.exp(scores - row_max)
    probs = shifted / lax.optimization_barrier(jnp.sum(shifted, axis=-1, keepdims=True))
    return jnp.einsum('hqk,khe->qhe', low(probs), value_heads, precision=HIGH)

def group_forward(params, block_rows):
    ln1_gain, ln1_bias, qkv_weight, qv_bias, proj_weight, proj_bias, ln2_gain, ln2_bias, fc1_weight, fc1_bias, fc2_weight, fc2_bias = params
    images = block_rows.shape[0] // SEQ
    normed_one = low(layer_norm(block_rows, ln1_gain, ln1_bias))
    projected = jnp.einsum('td,dcf->tcf', normed_one, qkv_weight, precision=HIGH)
    qv_flat = qv_bias.reshape(2, D)
    head_shape = (images, SEQ, HEADS, HD)
    queries = low_back(low(projected[:, 0] + qv_flat[0])).reshape(head_shape)
    key_heads = low_back(low(projected[:, 1])).reshape(head_shape)
    value_heads = low_back(low(projected[:, 2] + qv_flat[1])).reshape(head_shape)
    mixed = lax.map(jax.checkpoint(lambda image_set: attend_image(*image_set)), (queries, key_heads, value_heads))
    mixed = low_back(low(mixed.reshape(images * SEQ, D)))
    branch_one = low_back(matmul_high(mixed, proj_weight))
    residual = block_rows + branch_one + proj_bias
    normed_two = low(layer_norm(residual, ln2_gain, ln2_bias))
    hidden_pre = low_back(matmul_high(normed_two, fc1_weight) + fc1_bias.reshape(FF))
    hidden = low(gelu_exact(hidden_pre))
    branch_two = low_back(matmul_high(hidden, fc2_weight))
    return residual + branch_two + fc2_bias

def reference(tokens, ln1_gain, ln1_bias, qkv_weight, qv_bias, proj_weight, proj_bias, ln2_gain, ln2_bias, fc1_weight, fc1_bias, fc2_weight, fc2_bias, cotangent):
    params = tuple((member.astype(jnp.float32) for member in (ln1_gain, ln1_bias, qkv_weight, qv_bias, proj_weight, proj_bias, ln2_gain, ln2_bias, fc1_weight, fc1_bias, fc2_weight, fc2_bias)))
    blocks = tokens.astype(jnp.float32).reshape(N_DP, IMG_DEV * SEQ, D)

    def forward(params, blocks):

        def scan_step(carried, block_rows):
            return (carried, jax.checkpoint(group_forward)(params, block_rows))
        _, outputs = lax.scan(scan_step, jnp.zeros((), jnp.float32), blocks)
        return outputs
    outputs, pullback = jax.vjp(forward, params, blocks)
    param_grads, token_grads = pullback(cotangent.astype(jnp.float32).reshape(outputs.shape))
    g_ln1_gain, g_ln1_bias, g_qkv, g_qv, g_proj, g_proj_bias, g_ln2_gain, g_ln2_bias, g_fc1, g_fc1_bias, g_fc2, g_fc2_bias = param_grads
    return (outputs.reshape(TOKENS, D).astype(jnp.bfloat16), token_grads.reshape(TOKENS, D), g_ln1_gain, g_ln1_bias, g_qkv, g_qv, g_proj, g_proj_bias, g_ln2_gain, g_ln2_bias, g_fc1, g_fc1_bias, g_fc2, g_fc2_bias)
```

```python
import functools
import itertools
import math

import jax
import jax.numpy as jnp
import numpy as np
from jax import lax
from jax.experimental import pallas as pl
from jax.experimental.pallas import tpu as pltpu
from jax.sharding import Mesh
from jax.sharding import PartitionSpec as P

SEQ = 577
ROWS = 592
HEAD = 64
EPS = 1e-06
ALL = ("z", "x", "c", "y")
F32 = jnp.float32
BF16 = jnp.bfloat16

NN = (((1,), (0,)), ((), ()))
NT = (((1,), (1,)), ((), ()))
TN = (((0,), (0,)), ((), ()))
VMEM_LIMIT = 48 * 2**20


def dot(left, right, dims=NN):
    return lax.dot_general(left, right, dims, preferred_element_type=F32)


def attend_kernel(heads, qkv_ref, mixed_ref, probs_ref):
    width = heads * HEAD
    for pair in range(heads // 2):
        at = pair * 128
        queries = qkv_ref[:, at : at + 128]
        keys = qkv_ref[:, width + at : width + at + 128]
        values = qkv_ref[:, 2 * width + at : 2 * width + at + 128]
        lane = lax.broadcasted_iota(jnp.int32, (ROWS, 128), 1)
        row = lax.broadcasted_iota(jnp.int32, (ROWS, ROWS), 0)
        mixed = []
        for half in range(2):
            inside = (lane < HEAD) if half == 0 else (lane >= HEAD)
            own_keys = jnp.where(inside, keys, jnp.zeros_like(keys)) * BF16(0.125)
            scores = dot(own_keys, queries, NT)
            scores = jnp.where(row < SEQ, scores, -1e30)
            shifted = jnp.exp(scores - jnp.max(scores, axis=0, keepdims=True))
            total = jnp.sum(shifted, axis=0, keepdims=True)
            probs = (shifted * (1.0 / total)).astype(BF16)
            probs_ref[0, 2 * pair + half] = probs
            mixed.append(dot(probs, values, TN))
        mixed_ref[:, at : at + 128] = jnp.where(lane < HEAD, mixed[0], mixed[1]).astype(BF16)


def attend(projected, heads):
    width = heads * HEAD
    return pl.pallas_call(
        functools.partial(attend_kernel, heads),
        grid=(2,),
        in_specs=[pl.BlockSpec((ROWS, 3 * width), lambda i: (i, 0))],
        out_specs=[
            pl.BlockSpec((ROWS, width), lambda i: (i, 0)),
            pl.BlockSpec((1, heads, ROWS, ROWS), lambda i: (i, 0, 0, 0)),
        ],
        out_shape=[
            jax.ShapeDtypeStruct((2 * ROWS, width), BF16),
            jax.ShapeDtypeStruct((2, heads, ROWS, ROWS), BF16),
        ],
        compiler_params=pltpu.CompilerParams(vmem_limit_bytes=VMEM_LIMIT),
        cost_estimate=pl.CostEstimate(
            flops=12 * heads * ROWS * ROWS * 256,
            bytes_accessed=2 * 2 * heads * ROWS * (ROWS + 256),
            transcendentals=2 * heads * ROWS * ROWS,
        ),
    )(projected)


def attend_back_kernel(heads, qkv_ref, probs_ref, grad_ref, out_ref):
    width = heads * HEAD
    for pair in range(heads // 2):
        at = pair * 128
        queries = qkv_ref[:, at : at + 128]
        keys = qkv_ref[:, width + at : width + at + 128]
        values = qkv_ref[:, 2 * width + at : 2 * width + at + 128]
        grad = grad_ref[:, at : at + 128]
        lane = lax.broadcasted_iota(jnp.int32, (ROWS, 128), 1)
        keys_t = (keys * BF16(0.125)).T
        queries_s = queries * BF16(0.125)
        d_query, d_key, d_value = [], [], []
        for half in range(2):
            inside = (lane < HEAD) if half == 0 else (lane >= HEAD)
            own_values = jnp.where(inside, values, jnp.zeros_like(values))
            low_probs = probs_ref[0, 2 * pair + half]
            prob_grad = dot(own_values, grad, NT)
            probs = low_probs.astype(F32)
            product = prob_grad * probs
            weighted = jnp.sum(product, axis=0, keepdims=True)
            score_grad = (product - probs * weighted).astype(BF16)
            d_value.append(dot(low_probs, grad))
            d_key.append(dot(score_grad, queries_s))
            d_query.append(dot(keys_t[half * HEAD : (half + 1) * HEAD], score_grad))
        out_ref[:, at : at + 128] = jnp.concatenate(d_query, 0).T.astype(BF16)
        out_ref[:, width + at : width + at + 128] = jnp.where(
            lane < HEAD, d_key[0], d_key[1]
        ).astype(BF16)
        out_ref[:, 2 * width + at : 2 * width + at + 128] = jnp.where(
            lane < HEAD, d_value[0], d_value[1]
        ).astype(BF16)


def attend_back(projected, probs, mixed_grad, heads):
    width = heads * HEAD
    return pl.pallas_call(
        functools.partial(attend_back_kernel, heads),
        grid=(2,),
        in_specs=[
            pl.BlockSpec((ROWS, 3 * width), lambda i: (i, 0)),
            pl.BlockSpec((1, heads, ROWS, ROWS), lambda i: (i, 0, 0, 0)),
            pl.BlockSpec((ROWS, width), lambda i: (i, 0)),
        ],
        out_specs=pl.BlockSpec((ROWS, 3 * width), lambda i: (i, 0)),
        out_shape=jax.ShapeDtypeStruct((2 * ROWS, 3 * width), BF16),
        compiler_params=pltpu.CompilerParams(vmem_limit_bytes=VMEM_LIMIT),
        cost_estimate=pl.CostEstimate(
            flops=20 * heads * ROWS * ROWS * 256,
            bytes_accessed=2 * 2 * heads * ROWS * (ROWS + 448),
            transcendentals=0,
        ),
    )(projected, probs, mixed_grad)


def place(parts, spots, shape, block):
    def kernel(spot_ref, *refs):
        out_ref, sems = refs[-2], refs[-1]
        copies = []
        for n in range(len(parts)):
            copies.append(
                pltpu.make_async_copy(refs[n], block(out_ref, spot_ref[n]), sems.at[n])
            )
        for copy in copies:
            copy.start()
        for copy in copies:
            copy.wait()

    size = math.prod(shape) * 2
    return pl.pallas_call(
        kernel,
        grid_spec=pltpu.PrefetchScalarGridSpec(
            num_scalar_prefetch=1,
            grid=(1,),
            in_specs=[pl.BlockSpec(memory_space=pl.ANY)] * len(parts),
            out_specs=pl.BlockSpec(memory_space=pl.ANY),
            scratch_shapes=[pltpu.SemaphoreType.DMA((len(parts),))],
        ),
        out_shape=jax.ShapeDtypeStruct(shape, parts[0].dtype),
        compiler_params=pltpu.CompilerParams(vmem_limit_bytes=2**20),
        cost_estimate=pl.CostEstimate(flops=0, bytes_accessed=2 * size, transcendentals=0),
    )(spots, *parts)


def row_stats(values):
    mean = jnp.mean(values, axis=-1, keepdims=True)
    centered = values - mean
    inv = lax.rsqrt(jnp.mean(jnp.square(centered), axis=-1, keepdims=True) + EPS)
    return mean, inv


def norm_back(upstream, normed, inv_scale, gain):
    scaled = upstream * gain
    first = jnp.mean(scaled, axis=-1, keepdims=True)
    second = jnp.mean(scaled * normed, axis=-1, keepdims=True)
    return inv_scale * (scaled - first - normed * second)


def build(n_z, n_x):
    sizes = dict(z=n_z, x=n_x, c=2, y=2)

    def pairs(move, only=None):
        found = []
        names = ALL
        spots = list(itertools.product(*[range(sizes[a]) for a in names]))
        index = {spot: n for n, spot in enumerate(spots)}
        for spot in spots:
            here = dict(zip(names, spot))
            if only is not None and not only(here):
                continue
            there = dict(here)
            move(there)
            found.append((index[spot], index[tuple(there[a] for a in names)]))
        return found

    def shift(axis, by, only=None):
        def move(spot):
            spot[axis] = (spot[axis] + by) % sizes[axis]

        return pairs(move, only)

    def send(value, perm):
        return lax.ppermute(value, ALL, perm)

    def is_owner(spot):
        return spot["c"] == spot["y"]

    def not_owner(spot):
        return spot["c"] != spot["y"]

    def on_device(
        tokens,
        ln1_gain,
        ln1_bias,
        qkv_weight,
        qv_bias,
        proj_weight,
        proj_bias,
        ln2_gain,
        ln2_bias,
        fc1_weight,
        fc1_bias,
        fc2_weight,
        fc2_bias,
        cotangent,
    ):
        z, x, c, y = [lax.axis_index(a) for a in ALL]
        owner = c == y
        width = tokens.shape[1]
        depth = fc1_weight.shape[0]
        pair = 2 * depth
        heads = qv_bias.shape[1] // 2

        def swap(value):
            return send(value, shift("c", 1))

        def chunks(arrays):
            own = jnp.concatenate(arrays, axis=1)
            other = swap(own)
            both = jnp.where(c == 0, jnp.stack([own, other]), jnp.stack([other, own]))
            both = both.reshape(pair, own.shape[1])
            return both

        quarter = proj_weight.shape[0] // 2
        proj_t = proj_weight.T
        fc2_t = fc2_weight.T
        parts = []
        for colour in range(2):
            cut = slice(colour * quarter, (colour + 1) * quarter)
            parts += [qkv_weight[:, n, cut] for n in range(3)] + [proj_t[:, cut]]
        first = chunks(parts)
        span = 4 * quarter
        rest = chunks([fc1_weight, fc2_t])
        hidden_half = fc1_weight.shape[1] // 2
        groups = [
            (first[:, :span], first[:, span:]),
            (rest[:, :hidden_half], rest[:, hidden_half : 2 * hidden_half]),
            (rest[:, 2 * hidden_half : 3 * hidden_half], rest[:, 3 * hidden_half :]),
        ]

        z_spots = (z + jnp.arange(n_z, dtype=jnp.int32)) % n_z
        x_spots = (x + jnp.arange(n_x, dtype=jnp.int32)) % n_x

        def gather_a(chunk):
            wide = chunk.shape[1]
            moved = send(chunk, shift("y", 1, is_owner))
            chunk = jnp.where(owner, chunk, moved)
            bufs = [chunk]
            for _ in range(n_z - 1):
                bufs.append(send(bufs[-1], shift("z", -1)))
            column = place(bufs, z_spots, (n_z, pair, wide), lambda ref, n: ref.at[n])
            bufs = [column]
            for _ in range(n_x - 1):
                bufs.append(send(bufs[-1], shift("x", -1)))
            whole = place(bufs, x_spots, (n_z, n_x, pair, wide), lambda ref, n: ref.at[:, n])
            return whole.reshape(width, wide)

        def gather_b(chunk):
            wide = chunk.shape[1]
            bufs = [chunk]
            for _ in range(n_x - 1):
                bufs.append(send(bufs[-1], shift("x", -1, is_owner)))
            line = place(bufs, x_spots, (n_x, pair, wide), lambda ref, n: ref.at[n])
            bufs = [line]
            for _ in range(n_z - 1):
                bufs.append(send(bufs[-1], shift("z", -1, is_owner)))
            plane = place(bufs, z_spots, (n_z, n_x, pair, wide), lambda ref, n: ref.at[n])
            moved = send(plane, shift("y", 1, is_owner))
            return jnp.where(owner, plane, moved).reshape(width, wide)

        def add(left, right):
            return (left.astype(F32) + right.astype(F32)).astype(BF16)

        def finish(total):
            first, second = total[:depth], total[depth:]
            moved = swap(jnp.where(c == 0, second, first))
            kept = jnp.where(c == 0, first, second)
            return jnp.where(owner, kept, moved).astype(F32)

        def pick(array, axis, index):
            return lax.dynamic_index_in_dim(array, index, axis, keepdims=False)

        def scatter_a(grad):
            grad = grad.reshape(n_z, n_x, pair, grad.shape[1])
            total = pick(grad, 1, (x + n_x - 1) % n_x)
            for k in range(n_x - 2, -1, -1):
                total = add(send(total, shift("x", 1)), pick(grad, 1, (x + k) % n_x))
            lines = total
            total = pick(lines, 0, (z + n_z - 1) % n_z)
            for k in range(n_z - 2, -1, -1):
                total = add(send(total, shift("z", 1)), pick(lines, 0, (z + k) % n_z))
            return finish(add(send(total, shift("y", 1, not_owner)), total))

        def scatter_b(grad):
            grad = add(send(grad, shift("y", 1, not_owner)), grad)
            grad = grad.reshape(n_z, n_x, pair, grad.shape[1])
            total = pick(grad, 0, (z + n_z - 1) % n_z)
            for k in range(n_z - 2, -1, -1):
                total = add(send(total, shift("z", 1, is_owner)), pick(grad, 0, (z + k) % n_z))
            lines = total
            total = pick(lines, 0, (x + n_x - 1) % n_x)
            for k in range(n_x - 2, -1, -1):
                total = add(send(total, shift("x", 1, is_owner)), pick(lines, 0, (x + k) % n_x))
            return finish(total)

        small = jnp.concatenate(
            [ln1_gain, ln1_bias, ln2_gain, ln2_bias, proj_bias, fc2_bias]
            + [qv_bias.reshape(-1), fc1_bias.reshape(-1)]
        )[None]
        where_am_i = dict(z=z, x=x, c=c, y=y)
        for axis in ("c", "y", "x", "z"):
            count = sizes[axis]
            stacked = jnp.stack([small] + [send(small, shift(axis, -k)) for k in range(1, count)])
            start = (count - where_am_i[axis]) % count
            small = lax.dynamic_slice_in_dim(jnp.concatenate([stacked] * 2), start, count, 0)
        share = ln1_gain.shape[0]
        small = small.reshape(n_z, n_x, 2, 2, -1)
        small = small.transpose(0, 1, 3, 2, 4)
        vectors = small[..., : 6 * share].reshape(-1, 6, share).transpose(1, 0, 2).reshape(6, -1)
        gain_one, shift_one, gain_two, shift_two, proj_shift, out_shift = vectors.astype(F32)
        mine = pick(small[..., 6 * share :], 3, c).astype(F32)
        per_qv = qv_bias.shape[2]
        n_qv = qv_bias.size
        qv_half = mine[..., :n_qv].reshape((-1,) + qv_bias.shape)
        qv_half = qv_half.transpose(1, 2, 0, 3).reshape(2, -1)
        per_fc1 = fc1_bias.shape[1]
        fc1_half = mine[..., n_qv:].reshape((-1,) + fc1_bias.shape)
        fc1_half = fc1_half.transpose(1, 0, 2).reshape(-1)

        def both_images(value):
            value = jnp.pad(value, ((0, ROWS - SEQ), (0, 0)))
            return jnp.concatenate([value, swap(value)])

        inputs = both_images(tokens)
        down = both_images(cotangent)

        def own(value):
            return value[:ROWS]

        def exchanged(partial):
            moved = swap(partial.astype(BF16)).astype(F32)
            return partial + jnp.concatenate([moved[ROWS:], moved[:ROWS]])

        def exchanged_own(partial):
            return partial[:ROWS] + swap(partial[ROWS:].astype(BF16)).astype(F32)

        attn_a, attn_b = gather_a(groups[0][0]), gather_b(groups[0][1])
        fc1_a, fc1_b = gather_a(groups[1][0]), gather_b(groups[1][1])
        fc2_a, fc2_b = gather_a(groups[2][0]), gather_b(groups[2][1])
        n_qkv = 3 * quarter

        wide_in = inputs.astype(F32)
        mean_one, inv_one = row_stats(wide_in)
        hat_one = (wide_in - mean_one) * inv_one
        normed_one = (hat_one * gain_one + shift_one).astype(BF16)

        mixed, probs, projected = [], [], []
        for colour, weight in enumerate((attn_a, attn_b)):
            cut = slice(colour * quarter, (colour + 1) * quarter)
            bias = jnp.concatenate(
                [qv_half[0, cut], jnp.zeros((quarter,), F32), qv_half[1, cut]]
            )
            here = (dot(normed_one, weight[:, :n_qkv]) + bias).astype(BF16)
            out, prob = attend(here, heads)
            projected.append(here)
            mixed.append(out)
            probs.append(prob)
        proj_ab = [attn_a[:, n_qkv:], attn_b[:, n_qkv:]]
        branch_one = dot(mixed[0], proj_ab[0], NT) + dot(mixed[1], proj_ab[1], NT)
        residual = wide_in + exchanged(branch_one) + proj_shift
        mean_two, inv_two = row_stats(residual)
        hat_two = (residual - mean_two) * inv_two
        normed_two = (hat_two * gain_two + shift_two).astype(BF16)

        hidden, slope = [], []
        for colour, weight in enumerate((fc1_a, fc1_b)):
            bias = fc1_half[colour * hidden_half : (colour + 1) * hidden_half]
            pre = dot(normed_two, weight) + bias
            cdf = 0.5 * (1.0 + lax.erf(pre * (1.0 / math.sqrt(2.0))))
            density = jnp.exp(-0.5 * pre * pre) * (1.0 / math.sqrt(2.0 * math.pi))
            hidden.append((pre * cdf).astype(BF16))
            slope.append((cdf + pre * density).astype(BF16))

        grad_fc2 = [dot(down, h, TN).astype(BF16) for h in hidden]
        scat_fc2 = [scatter_a(grad_fc2[0]), scatter_b(grad_fc2[1])]
        hidden_grad = [
            (dot(down, w) * s.astype(F32)).astype(BF16) for w, s in zip((fc2_a, fc2_b), slope)
        ]
        back_two = exchanged(dot(hidden_grad[0], fc1_a, NT) + dot(hidden_grad[1], fc1_b, NT))
        grad_fc1 = [dot(normed_two, g, TN).astype(BF16) for g in hidden_grad]
        scat_fc1 = [scatter_a(grad_fc1[0]), scatter_b(grad_fc1[1])]
        grad_fc1_shift = jnp.concatenate([jnp.sum(g.astype(F32), axis=0) for g in hidden_grad])

        branch_two = dot(hidden[0], fc2_a, NT) + dot(hidden[1], fc2_b, NT)
        output = (own(residual) + exchanged_own(branch_two) + out_shift).astype(BF16)[:SEQ]

        upstream = down.astype(F32)
        resid_grad = upstream + norm_back(back_two, hat_two, inv_two, gain_two)
        attn_grad = resid_grad.astype(BF16)

        parts, back_one, grad_qv = [], [], []
        for colour, weight in enumerate((attn_a, attn_b)):
            mixed_grad = dot(attn_grad, weight[:, n_qkv:]).astype(BF16)
            qkv_grad = attend_back(projected[colour], probs[colour], mixed_grad, heads)
            grad_qkv = dot(normed_one, qkv_grad, TN).astype(BF16)
            grad_proj = dot(attn_grad, mixed[colour], TN).astype(BF16)
            parts.append(jnp.concatenate([grad_qkv, grad_proj], axis=1))
            back_one.append(dot(qkv_grad, weight[:, :n_qkv], NT))
            grad_qv.append(jnp.sum(qkv_grad.astype(F32), axis=0))
        scat_attn = [scatter_a(parts[0]), scatter_b(parts[1])]
        back_one = exchanged_own(back_one[0] + back_one[1])
        hat_own = own(hat_one)
        grad_tokens = own(resid_grad) + norm_back(back_one, hat_own, own(inv_one), gain_one)

        six = [
            jnp.sum(back_one * hat_own, axis=0),
            jnp.sum(back_one, axis=0),
            jnp.sum(own(back_two) * own(hat_two), axis=0),
            jnp.sum(own(back_two), axis=0),
            jnp.sum(own(resid_grad), axis=0),
            jnp.sum(own(upstream), axis=0),
        ]
        halves = [g[:quarter] for g in grad_qv] + [g[2 * quarter :] for g in grad_qv]
        sums = jnp.concatenate(six + halves + [grad_fc1_shift])[None]
        for axis in ("z", "x", "y"):
            moved = [send(sums, shift(axis, k)) for k in range(1, sizes[axis])]
            sums = functools.reduce(jnp.add, moved, sums)
        moved = swap(sums)[0]
        sums = sums[0]
        spot = ((z * n_x + x) * 2 + c) * 2 + y
        small_own = (sums[: 6 * width] + moved[: 6 * width]).reshape(6, -1, share)
        small_own = pick(small_own, 1, spot)
        half = jnp.where(owner, sums[6 * width :], moved[6 * width :])
        deep = (z * n_x + x) * 2 + c
        grad_qv = half[: 4 * quarter].reshape(2, qv_bias.shape[1], -1, per_qv)
        grad_qv = pick(grad_qv, 2, deep)
        grad_fc1_bias = pick(half[4 * quarter :].reshape(fc1_bias.shape[0], -1, per_fc1), 1, deep)

        def joined(index):
            cut = slice(index * quarter, (index + 1) * quarter)
            return jnp.concatenate([s[:, cut] for s in scat_attn], axis=1)

        grad_qkv = jnp.stack([joined(0), joined(1), joined(2)], axis=1)
        return (
            output,
            grad_tokens[:SEQ],
            small_own[0],
            small_own[1],
            grad_qkv,
            grad_qv,
            joined(3).T,
            small_own[4],
            small_own[2],
            small_own[3],
            jnp.concatenate(scat_fc1, axis=1),
            grad_fc1_bias,
            jnp.concatenate(scat_fc2, axis=1).T,
            small_own[5],
        )

    return on_device


def solution(mesh):
    chips = mesh.shape["dp"] // 2
    n_x = 1
    while n_x * n_x * 4 <= chips and chips % (n_x * 2) == 0:
        n_x *= 2
    n_z = chips // n_x
    fine = Mesh(np.asarray(mesh.devices).reshape(n_z, n_x, 2, 2), ALL)
    dp = ("z", "x", "c")
    every = P(ALL)
    rows = P(ALL, None)
    in_specs = (
        rows,
        every,
        every,
        P(dp, None, "y"),
        P(None, "y", dp),
        P("y", dp),
        every,
        every,
        every,
        P(dp, "y"),
        P("y", dp),
        P("y", dp),
        every,
        rows,
    )
    out_specs = (
        rows,
        rows,
        every,
        every,
        P(dp, None, "y"),
        P(None, "y", dp),
        P("y", dp),
        every,
        every,
        every,
        P(dp, "y"),
        P("y", dp),
        P("y", dp),
        every,
    )
    return jax.shard_map(
        build(n_z, n_x), mesh=fine, in_specs=in_specs, out_specs=out_specs, check_vma=False
    )
```

```python
import functools
import itertools
import math

import jax
import jax.numpy as jnp
import numpy as np
from jax import lax
from jax.experimental import pallas as pl
from jax.experimental.pallas import tpu as pltpu
from jax.experimental.layout import Layout, with_layout_constraint
from jax.sharding import Mesh
from jax.sharding import PartitionSpec as P

SEQ = 577
ROWS = 592
HEAD = 64
EPS = 1e-06
ALL = ("z", "x", "c", "y")
F32 = jnp.float32
BF16 = jnp.bfloat16

NN = (((1,), (0,)), ((), ()))
NT = (((1,), (1,)), ((), ()))
TN = (((0,), (0,)), ((), ()))
VMEM_LIMIT = 48 * 2**20
LITTLE = pl.CostEstimate(flops=2**20, bytes_accessed=2**18, transcendentals=0)
LONG = pl.CostEstimate(flops=2**36, bytes_accessed=2**18, transcendentals=0)


def rows_first(array):
    return with_layout_constraint(array, Layout(major_to_minor=(0, 1)))


def dot(left, right, dims=NN):
    return lax.dot_general(left, right, dims, preferred_element_type=F32)


def attend_kernel(heads, qkv_ref, mixed_ref, probs_ref):
    width = heads * HEAD
    for pair in range(heads // 2):
        at = pair * 128
        queries = qkv_ref[:, at : at + 128]
        keys = qkv_ref[:, width + at : width + at + 128]
        values = qkv_ref[:, 2 * width + at : 2 * width + at + 128]
        lane = lax.broadcasted_iota(jnp.int32, (ROWS, 128), 1)
        row = lax.broadcasted_iota(jnp.int32, (ROWS, ROWS), 0)
        mixed = []
        for half in range(2):
            inside = (lane < HEAD) if half == 0 else (lane >= HEAD)
            own_keys = jnp.where(inside, keys, jnp.zeros_like(keys)) * BF16(0.125)
            scores = dot(own_keys, queries, NT)
            scores = jnp.where(row < SEQ, scores, -1e30)
            shifted = jnp.exp(scores - jnp.max(scores, axis=0, keepdims=True))
            total = jnp.sum(shifted, axis=0, keepdims=True)
            probs = (shifted * (1.0 / total)).astype(BF16)
            probs_ref[0, 2 * pair + half] = probs
            mixed.append(dot(probs, values, TN))
        mixed_ref[:, at : at + 128] = jnp.where(lane < HEAD, mixed[0], mixed[1]).astype(BF16)


def attend(projected, heads):
    width = heads * HEAD
    return pl.pallas_call(
        functools.partial(attend_kernel, heads),
        grid=(2,),
        in_specs=[pl.BlockSpec((ROWS, 3 * width), lambda i: (i, 0))],
        out_specs=[
            pl.BlockSpec((ROWS, width), lambda i: (i, 0)),
            pl.BlockSpec((1, heads, ROWS, ROWS), lambda i: (i, 0, 0, 0)),
        ],
        out_shape=[
            jax.ShapeDtypeStruct((2 * ROWS, width), BF16),
            jax.ShapeDtypeStruct((2, heads, ROWS, ROWS), BF16),
        ],
        compiler_params=pltpu.CompilerParams(vmem_limit_bytes=VMEM_LIMIT),
        cost_estimate=LONG,
    )(projected)


def attend_back_kernel(heads, qkv_ref, probs_ref, grad_ref, out_ref):
    width = heads * HEAD
    for pair in range(heads // 2):
        at = pair * 128
        queries = qkv_ref[:, at : at + 128]
        keys = qkv_ref[:, width + at : width + at + 128]
        values = qkv_ref[:, 2 * width + at : 2 * width + at + 128]
        grad = grad_ref[:, at : at + 128]
        lane = lax.broadcasted_iota(jnp.int32, (ROWS, 128), 1)
        keys_t = (keys * BF16(0.125)).T
        queries_s = queries * BF16(0.125)
        d_query, d_key, d_value = [], [], []
        for half in range(2):
            inside = (lane < HEAD) if half == 0 else (lane >= HEAD)
            own_values = jnp.where(inside, values, jnp.zeros_like(values))
            low_probs = probs_ref[0, 2 * pair + half]
            prob_grad = dot(own_values, grad, NT)
            probs = low_probs.astype(F32)
            product = prob_grad * probs
            weighted = jnp.sum(product, axis=0, keepdims=True)
            score_grad = (product - probs * weighted).astype(BF16)
            d_value.append(dot(low_probs, grad))
            d_key.append(dot(score_grad, queries_s))
            d_query.append(dot(keys_t[half * HEAD : (half + 1) * HEAD], score_grad))
        out_ref[:, at : at + 128] = jnp.concatenate(d_query, 0).T.astype(BF16)
        out_ref[:, width + at : width + at + 128] = jnp.where(
            lane < HEAD, d_key[0], d_key[1]
        ).astype(BF16)
        out_ref[:, 2 * width + at : 2 * width + at + 128] = jnp.where(
            lane < HEAD, d_value[0], d_value[1]
        ).astype(BF16)


def attend_back(projected, probs, mixed_grad, heads):
    width = heads * HEAD
    return pl.pallas_call(
        functools.partial(attend_back_kernel, heads),
        grid=(2,),
        in_specs=[
            pl.BlockSpec((ROWS, 3 * width), lambda i: (i, 0)),
            pl.BlockSpec((1, heads, ROWS, ROWS), lambda i: (i, 0, 0, 0)),
            pl.BlockSpec((ROWS, width), lambda i: (i, 0)),
        ],
        out_specs=pl.BlockSpec((ROWS, 3 * width), lambda i: (i, 0)),
        out_shape=jax.ShapeDtypeStruct((2 * ROWS, 3 * width), BF16),
        compiler_params=pltpu.CompilerParams(vmem_limit_bytes=VMEM_LIMIT),
        cost_estimate=LONG,
    )(projected, probs, mixed_grad)


def place(parts, spots, shape, block):
    def kernel(spot_ref, *refs):
        out_ref, sems = refs[-2], refs[-1]
        copies = []
        for n in range(len(parts)):
            copies.append(
                pltpu.make_async_copy(refs[n], block(out_ref, spot_ref[n]), sems.at[n])
            )
        for copy in copies:
            copy.start()
        for copy in copies:
            copy.wait()

    return pl.pallas_call(
        kernel,
        grid_spec=pltpu.PrefetchScalarGridSpec(
            num_scalar_prefetch=1,
            grid=(1,),
            in_specs=[pl.BlockSpec(memory_space=pl.ANY)] * len(parts),
            out_specs=pl.BlockSpec(memory_space=pl.ANY),
            scratch_shapes=[pltpu.SemaphoreType.DMA((len(parts),))],
        ),
        out_shape=jax.ShapeDtypeStruct(shape, parts[0].dtype),
        compiler_params=pltpu.CompilerParams(vmem_limit_bytes=2**20),
        cost_estimate=LITTLE,
    )(spots, *parts)


def pack(qkv, proj, quarter):
    def kernel(qkv_ref, proj_ref, out_ref):
        for colour in range(2):
            cut = slice(colour * quarter, (colour + 1) * quarter)
            for n in range(4):
                at = (4 * colour + n) * quarter
                part = qkv_ref[n, :, cut] if n < 3 else proj_ref[:, cut]
                out_ref[:, at : at + quarter] = part

    return pl.pallas_call(
        kernel,
        out_shape=jax.ShapeDtypeStruct((proj.shape[0], 8 * quarter), proj.dtype),
        compiler_params=pltpu.CompilerParams(vmem_limit_bytes=VMEM_LIMIT),
        cost_estimate=LITTLE,
    )(qkv, proj)


def row_stats(values):
    mean = jnp.mean(values, axis=-1, keepdims=True)
    centered = values - mean
    inv = lax.rsqrt(jnp.mean(jnp.square(centered), axis=-1, keepdims=True) + EPS)
    return mean, inv


def norm_back(upstream, normed, inv_scale, gain):
    scaled = upstream * gain
    first = jnp.mean(scaled, axis=-1, keepdims=True)
    second = jnp.mean(scaled * normed, axis=-1, keepdims=True)
    return inv_scale * (scaled - first - normed * second)


def build(n_z, n_x):
    sizes = dict(z=n_z, x=n_x, c=2, y=2)

    def pairs(move, only=None):
        found = []
        names = ALL
        spots = list(itertools.product(*[range(sizes[a]) for a in names]))
        index = {spot: n for n, spot in enumerate(spots)}
        for spot in spots:
            here = dict(zip(names, spot))
            if only is not None and not only(here):
                continue
            there = dict(here)
            move(there)
            found.append((index[spot], index[tuple(there[a] for a in names)]))
        return found

    def shift(axis, by, only=None):
        def move(spot):
            spot[axis] = (spot[axis] + by) % sizes[axis]

        return pairs(move, only)

    def send(value, perm):
        return lax.ppermute(value, ALL, perm)

    def exchange(spot):
        spot["c"], spot["y"] = spot["y"], spot["c"]

    transpose = pairs(exchange)

    def on_device(
        tokens,
        ln1_gain,
        ln1_bias,
        qkv_weight,
        qv_bias,
        proj_weight,
        proj_bias,
        ln2_gain,
        ln2_bias,
        fc1_weight,
        fc1_bias,
        fc2_weight,
        fc2_bias,
        cotangent,
    ):
        z, x, c, y = [lax.axis_index(a) for a in ALL]
        owner = c == y
        where_am_i = dict(z=z, x=x, c=c, y=y)
        width = tokens.shape[1]
        depth = fc1_weight.shape[0]
        heads = qv_bias.shape[1] // 2

        def swap(value):
            return send(value, shift("c", 1))

        def after(value, *earlier):
            return lax.optimization_barrier((value,) + earlier)[0]

        quarter = proj_weight.shape[0] // 2
        hidden_half = fc1_weight.shape[1] // 2
        n_qkv = 3 * quarter
        proj_t = proj_weight.T
        fc2_t = fc2_weight.T
        shards = [pack(qkv_weight.transpose(1, 0, 2), proj_t, quarter), fc1_weight, fc2_t]

        def spots(axis):
            count = sizes[axis]
            return (where_am_i[axis] + jnp.arange(count, dtype=jnp.int32)) % count

        def from_all(value, axis, shape, block, earlier=()):
            moved = [send(value, shift(axis, -k)) for k in range(1, sizes[axis])]
            if earlier:
                moved = [after(part, *earlier) for part in moved]
            return place([value] + moved, spots(axis), shape, block)

        def crossed(shard):
            return send(shard, transpose)

        def halves(line):
            wide = line.shape[2] // 2
            return line[:, :, :wide], line[:, :, wide:]

        def step_one(first, second, *earlier):
            at = (n_z, n_x, depth, first.shape[2])
            first = from_all(first, "x", at, lambda ref, n: ref.at[:, n], earlier)
            at = (n_z, 2, depth, second.shape[2])
            return first, from_all(second, "y", at, lambda ref, n: ref.at[:, n], earlier)

        def step_two(first, second, *earlier):
            wide = first.shape[3]
            at = (n_z, n_x, 2, depth, wide)
            first = from_all(first, "y", at, lambda ref, n: ref.at[:, :, n], earlier)
            second = from_all(second, "x", at, lambda ref, n: ref.at[:, n], earlier)
            return first.reshape(width, wide), second.reshape(width, wide)

        def pick(array, axis, index):
            return lax.dynamic_index_in_dim(array, index, axis, keepdims=False)

        def give(array, axis, dim):
            count, here = sizes[axis], where_am_i[axis]
            moved = [
                send(pick(array, dim, (here + k) % count), shift(axis, k))
                for k in range(1, count)
            ]
            return moved, pick(array, dim, here)

        def summed(given, *earlier):
            moved, own_part = given
            total = own_part.astype(F32)
            for part in moved:
                total = total + (after(part, *earlier) if earlier else part).astype(F32)
            return total.astype(BF16)

        def scatter_one(first, second):
            at = (n_z, n_x, 2, depth, first.shape[1])
            return give(first.reshape(at), "y", 2), give(second.reshape(at), "x", 1)

        def scatter_two(first, second):
            return give(first, "x", 1), give(second, "y", 1)

        def scatter_three(first, second):
            both = jnp.concatenate([first, second], axis=2)
            own = lax.psum_scatter(both, "z", scatter_dimension=0, tiled=False)
            return send(own, transpose)

        shard_one = crossed(shards[0])
        shard_two = crossed(after(shards[1], shard_one))
        shard_three = crossed(after(shards[2], shard_one))
        shard_one = after(shard_one, shard_two, shard_three)
        wide = shards[0].shape[1] // 2
        around = [shard_one] + [send(shard_one, shift("z", -k)) for k in range(1, n_z)]
        line_one = [
            place(
                [part[:, cut] for part in around],
                spots("z"),
                (n_z, depth, wide),
                lambda ref, n: ref.at[n],
            )
            for cut in (slice(0, wide), slice(wide, 2 * wide))
        ]
        line_two = lax.all_gather(after(shard_two, around[1]), "z", axis=0)
        line_three = lax.all_gather(after(shard_three, line_two), "z", axis=0)

        small = jnp.concatenate(
            [after(ln1_gain, around[1]), ln1_bias, ln2_gain, ln2_bias, proj_bias, fc2_bias]
            + [qv_bias.reshape(-1), fc1_bias.reshape(-1)]
        )[None]
        for axis in ("c", "y", "x", "z"):
            count = sizes[axis]
            stacked = jnp.stack([small] + [send(small, shift(axis, -k)) for k in range(1, count)])
            start = (count - where_am_i[axis]) % count
            small = lax.dynamic_slice_in_dim(jnp.concatenate([stacked] * 2), start, count, 0)
        share = ln1_gain.shape[0]
        small = small.reshape(n_z, n_x, 2, 2, -1)
        small = small.transpose(0, 1, 3, 2, 4)
        vectors = small[..., : 6 * share].reshape(-1, 6, share).transpose(1, 0, 2).reshape(6, -1)
        gain_one, shift_one, gain_two, shift_two, proj_shift, out_shift = vectors.astype(F32)
        mine = pick(small[..., 6 * share :], 3, c).astype(F32)
        per_qv = qv_bias.shape[2]
        n_qv = qv_bias.size
        qv_half = mine[..., :n_qv].reshape((-1,) + qv_bias.shape)
        qv_half = qv_half.transpose(1, 2, 0, 3).reshape(2, -1)
        per_fc1 = fc1_bias.shape[1]
        fc1_half = mine[..., n_qv:].reshape((-1,) + fc1_bias.shape)
        fc1_half = fc1_half.transpose(1, 0, 2).reshape(-1)

        def both_images(value):
            value = jnp.pad(value, ((0, ROWS - SEQ), (0, 0)))
            return jnp.concatenate([value, swap(value)])

        inputs = both_images(after(tokens, around[1]))

        def own(value):
            return value[:ROWS]

        def exchanged(partial, low, *earlier):
            moved = swap(low)
            moved = (after(moved, *earlier) if earlier else moved).astype(F32)
            return partial + jnp.concatenate([moved[ROWS:], moved[:ROWS]])

        def exchanged_own(partial):
            return partial[:ROWS] + swap(partial[ROWS:].astype(BF16)).astype(F32)

        square_one = step_one(*line_one)
        wide_in = inputs.astype(F32)
        mean_one, inv_one = row_stats(wide_in)
        hat_one = (wide_in - mean_one) * inv_one
        normed_one = (hat_one * gain_one + shift_one).astype(BF16)
        down = both_images(after(cotangent, normed_one))

        attn_w = step_two(*square_one, normed_one)
        half_two = [after(v, *square_one) for v in halves(line_two)]
        projected, probs, mixed = [None] * 2, [None] * 2, [None] * 2

        def attend_half(colour, rows):
            cut = slice(colour * quarter, (colour + 1) * quarter)
            bias = jnp.concatenate(
                [qv_half[0, cut], jnp.zeros((quarter,), F32), qv_half[1, cut]]
            )
            here = (dot(rows, attn_w[colour][:, :n_qkv]) + bias).astype(BF16)
            projected[colour] = here
            mixed[colour], probs[colour] = attend(here, heads)

        attend_half(0, after(normed_one, *half_two))
        square_two = step_one(*half_two, mixed[0])
        half_three = [after(v, *square_two) for v in halves(line_three)]
        attend_half(1, after(normed_one, *half_three))
        proj_ab = [w[:, n_qkv:] for w in attn_w]
        branch_one = dot(mixed[0], proj_ab[0], NT) + dot(mixed[1], proj_ab[1], NT)
        branch_low = branch_one.astype(BF16)
        fc1_w = step_two(*square_two, branch_low)
        residual = wide_in + exchanged(branch_one, branch_low) + proj_shift
        mean_two, inv_two = row_stats(residual)
        hat_two = (residual - mean_two) * inv_two
        normed_two = (hat_two * gain_two + shift_two).astype(BF16)
        square_three = step_one(*half_three, normed_two)

        hidden, slope = [], []
        rows_two = after(normed_two, *square_three)
        for colour, weight in enumerate(fc1_w):
            bias = fc1_half[colour * hidden_half : (colour + 1) * hidden_half]
            pre = dot(rows_two, weight) + bias
            cdf = 0.5 * (1.0 + lax.erf(pre * (1.0 / math.sqrt(2.0))))
            density = jnp.exp(-0.5 * pre * pre) * (1.0 / math.sqrt(2.0 * math.pi))
            hidden.append((pre * cdf).astype(BF16))
            slope.append((cdf + pre * density).astype(BF16))

        grad_fc2 = [rows_first(dot(down, h, TN).astype(BF16)) for h in hidden]
        fc2_one = scatter_one(*grad_fc2)
        fc2_w = step_two(*square_three, *grad_fc2)
        down_late = after(down, *grad_fc2)
        hidden_grad = [
            (dot(down_late, w) * s.astype(F32)).astype(BF16) for w, s in zip(fc2_w, slope)
        ]
        back_two = dot(hidden_grad[0], fc1_w[0], NT) + dot(hidden_grad[1], fc1_w[1], NT)
        back_low = back_two.astype(BF16)
        fc2_sums = [summed(given, back_low) for given in fc2_one]
        fc2_two = scatter_two(*fc2_sums)
        normed_late = after(normed_two, *fc2_sums)
        grad_fc1 = [rows_first(dot(normed_late, g, TN).astype(BF16)) for g in hidden_grad]
        grad_fc1_shift = jnp.concatenate([jnp.sum(g.astype(F32), axis=0) for g in hidden_grad])
        fc1_one = scatter_one(*grad_fc1)

        upstream = down.astype(F32)
        back_two = exchanged(back_two, back_low, *grad_fc1)
        resid_grad = upstream + norm_back(back_two, hat_two, inv_two, gain_two)
        attn_grad = resid_grad.astype(BF16)

        mixed_grad = [dot(attn_grad, w).astype(BF16) for w in proj_ab]
        fc2_lines = [summed(given, *mixed_grad) for given in fc2_two]
        scat_fc2 = scatter_three(*fc2_lines)

        def attn_grads(colour, qkv_grad, *earlier):
            rows, top = after(normed_one, *earlier), after(attn_grad, *earlier)
            grad_qkv = dot(rows, qkv_grad, TN).astype(BF16)
            grad_proj = dot(top, mixed[colour], TN).astype(BF16)
            cut = 2 * quarter
            return (
                rows_first(grad_qkv[:, :cut]),
                rows_first(jnp.concatenate([grad_qkv[:, cut:], grad_proj], axis=1)),
            )

        back_a = attend_back(after(projected[0], *fc2_lines), probs[0], mixed_grad[0], heads)
        fc1_sums = [summed(given, back_a) for given in fc1_one]
        fc1_two = scatter_two(*fc1_sums)
        grads_a = attn_grads(0, back_a, *fc1_sums)
        a_one = scatter_one(*grads_a)
        back_b = attend_back(after(projected[1], *grads_a), probs[1], mixed_grad[1], heads)
        fc1_lines = [summed(given, back_b) for given in fc1_two]
        scat_fc1 = scatter_three(*fc1_lines)
        a_sums = [summed(given, *fc1_lines) for given in a_one]
        a_two = scatter_two(*a_sums)
        grads_b = attn_grads(1, back_b, *a_sums)
        b_one = scatter_one(*grads_b)
        a_lines = [summed(given, *grads_b) for given in a_two]
        scat_a = scatter_three(*a_lines)
        qkv_grads = [after(g, *a_lines) for g in (back_a, back_b)]
        back_one = [dot(g, w[:, :n_qkv], NT) for g, w in zip(qkv_grads, attn_w)]
        back_one = back_one[0] + back_one[1]
        b_sums = [summed(given, back_one) for given in b_one]
        b_two = scatter_two(*b_sums)
        back_one = exchanged_own(after(back_one, *b_sums))
        grad_qv = [jnp.sum(g.astype(F32), axis=0) for g in qkv_grads]
        hat_own = own(hat_one)
        grad_tokens = own(resid_grad) + norm_back(back_one, hat_own, own(inv_one), gain_one)
        b_lines = [summed(given, back_one) for given in b_two]
        scat_b = scatter_three(*b_lines)
        scat_attn = jnp.concatenate([scat_a, scat_b], axis=1).astype(F32)

        hidden_late = [after(h, *b_lines) for h in hidden]
        branch_two = dot(hidden_late[0], fc2_w[0], NT) + dot(hidden_late[1], fc2_w[1], NT)
        output = (own(residual) + exchanged_own(branch_two) + out_shift).astype(BF16)[:SEQ]

        six = [
            jnp.sum(back_one * hat_own, axis=0),
            jnp.sum(back_one, axis=0),
            jnp.sum(own(back_two) * own(hat_two), axis=0),
            jnp.sum(own(back_two), axis=0),
            jnp.sum(own(resid_grad), axis=0),
            jnp.sum(own(upstream), axis=0),
        ]
        halves = [g[:quarter] for g in grad_qv] + [g[2 * quarter :] for g in grad_qv]
        sums = jnp.concatenate(six + halves + [grad_fc1_shift])[None]
        for axis in ("z", "x", "y"):
            moved = [send(sums, shift(axis, k)) for k in range(1, sizes[axis])]
            sums = functools.reduce(jnp.add, moved, sums)
        moved = swap(sums)[0]
        sums = sums[0]
        spot = ((z * n_x + x) * 2 + c) * 2 + y
        small_own = (sums[: 6 * width] + moved[: 6 * width]).reshape(6, -1, share)
        small_own = pick(small_own, 1, spot)
        half = jnp.where(owner, sums[6 * width :], moved[6 * width :])
        deep = (z * n_x + x) * 2 + c
        grad_qv = half[: 4 * quarter].reshape(2, qv_bias.shape[1], -1, per_qv)
        grad_qv = pick(grad_qv, 2, deep)
        grad_fc1_bias = pick(half[4 * quarter :].reshape(fc1_bias.shape[0], -1, per_fc1), 1, deep)

        def joined(index):
            at = index * quarter
            cuts = [scat_attn[:, at + half : at + half + quarter] for half in (0, 4 * quarter)]
            return jnp.concatenate(cuts, axis=1)

        grad_qkv = jnp.stack([joined(0), joined(1), joined(2)], axis=1)
        return (
            output,
            grad_tokens[:SEQ],
            small_own[0],
            small_own[1],
            grad_qkv,
            grad_qv,
            joined(3).T,
            small_own[4],
            small_own[2],
            small_own[3],
            scat_fc1.astype(F32),
            grad_fc1_bias,
            scat_fc2.astype(F32).T,
            small_own[5],
        )

    return on_device


def solution(mesh):
    chips = mesh.shape["dp"] // 2
    n_x = 1
    while n_x * n_x * 4 <= chips and chips % (n_x * 2) == 0:
        n_x *= 2
    n_z = chips // n_x
    fine = Mesh(np.asarray(mesh.devices).reshape(n_z, n_x, 2, 2), ALL)
    dp = ("z", "x", "c")
    every = P(ALL)
    rows = P(ALL, None)
    in_specs = (
        rows,
        every,
        every,
        P(dp, None, "y"),
        P(None, "y", dp),
        P("y", dp),
        every,
        every,
        every,
        P(dp, "y"),
        P("y", dp),
        P("y", dp),
        every,
        rows,
    )
    out_specs = (
        rows,
        rows,
        every,
        every,
        P(dp, None, "y"),
        P(None, "y", dp),
        P("y", dp),
        every,
        every,
        every,
        P(dp, "y"),
        P("y", dp),
        P("y", dp),
        every,
    )
    return jax.shard_map(
        build(n_z, n_x), mesh=fine, in_specs=in_specs, out_specs=out_specs, check_vma=False
    )
```

```python
import functools
import itertools
import math

import jax
import jax.numpy as jnp
import numpy as np
from jax import lax
from jax.experimental import pallas as pl
from jax.experimental.pallas import tpu as pltpu
from jax.experimental.layout import Layout, with_layout_constraint
from jax.sharding import Mesh
from jax.sharding import PartitionSpec as P

SEQ = 577
ROWS = 592
HEAD = 64
EPS = 1e-06
ALL = ("z", "x", "c", "y")
F32 = jnp.float32
BF16 = jnp.bfloat16

NN = (((1,), (0,)), ((), ()))
NT = (((1,), (1,)), ((), ()))
TN = (((0,), (0,)), ((), ()))
VMEM_LIMIT = 48 * 2**20
LITTLE = pl.CostEstimate(flops=2**20, bytes_accessed=2**18, transcendentals=0)


def rows_first(array):
    return with_layout_constraint(array, Layout(major_to_minor=(0, 1)))


def dot(left, right, dims=NN):
    return lax.dot_general(left, right, dims, preferred_element_type=F32)


def call(kernel, grid, ins, outs, *arrays):
    return pl.pallas_call(
        kernel,
        grid=grid,
        in_specs=[pl.BlockSpec(block, at) for block, at in ins],
        out_specs=[pl.BlockSpec(block, at) for block, at, _, _ in outs],
        out_shape=[jax.ShapeDtypeStruct(shape, dtype) for _, _, shape, dtype in outs],
        compiler_params=pltpu.CompilerParams(vmem_limit_bytes=VMEM_LIMIT),
        cost_estimate=LITTLE,
    )(*arrays)


def image(width):
    return (ROWS, width), lambda i: (i, 0)


def other_image(width):
    return (ROWS, width), lambda i: (1 - i, 0)


def fixed(*block):
    return block, lambda *i: (0,) * len(block)


def row_stats(values):
    mean = jnp.mean(values, axis=-1, keepdims=True)
    centered = values - mean
    inv = lax.rsqrt(jnp.mean(jnp.square(centered), axis=-1, keepdims=True) + EPS)
    return centered * inv, inv


def norm_back(upstream, normed, inv_scale, gain):
    scaled = upstream * gain
    first = jnp.mean(scaled, axis=-1, keepdims=True)
    second = jnp.mean(scaled * normed, axis=-1, keepdims=True)
    return inv_scale * (scaled - first - normed * second)


def norm_one(tokens, vectors):
    width = tokens.shape[1]

    def kernel(tokens_ref, vec_ref, out_ref):
        hat, _ = row_stats(tokens_ref[...].astype(F32))
        out_ref[...] = (hat * vec_ref[0:1] + vec_ref[1:2]).astype(BF16)

    out = image(width) + (tokens.shape, BF16)
    return call(kernel, (2,), [image(width), fixed(8, width)], [out], tokens, vectors)[0]


def attend(projected, heads):
    width = heads * HEAD

    def kernel(qkv_ref, mixed_ref, probs_ref):
        lane = lax.broadcasted_iota(jnp.int32, (ROWS, 128), 1)
        row = lax.broadcasted_iota(jnp.int32, (ROWS, ROWS), 0)
        for pair in range(heads // 2):
            at = pair * 128
            queries = qkv_ref[:, at : at + 128]
            keys = qkv_ref[:, width + at : width + at + 128]
            values = qkv_ref[:, 2 * width + at : 2 * width + at + 128]
            mixed = []
            for half in range(2):
                inside = (lane < HEAD) if half == 0 else (lane >= HEAD)
                own_keys = jnp.where(inside, keys, jnp.zeros_like(keys)) * BF16(0.125)
                scores = dot(own_keys, queries, NT)
                scores = jnp.where(row < SEQ, scores, -1e30)
                shifted = jnp.exp(scores - jnp.max(scores, axis=0, keepdims=True))
                total = jnp.sum(shifted, axis=0, keepdims=True)
                probs = (shifted * (1.0 / total)).astype(BF16)
                probs_ref[0, 2 * pair + half] = probs
                mixed.append(dot(probs, values, TN))
            mixed_ref[:, at : at + 128] = jnp.where(lane < HEAD, mixed[0], mixed[1]).astype(BF16)

    rows = 2 * ROWS
    return call(
        kernel,
        (2,),
        [image(3 * width)],
        [
            image(width) + ((rows, width), BF16),
            ((1, heads, ROWS, ROWS), lambda i: (i, 0, 0, 0), (2, heads, ROWS, ROWS), BF16),
        ],
        projected,
    )


def attend_back(projected, probs, mixed_grad, heads):
    width = heads * HEAD

    def kernel(qkv_ref, probs_ref, grad_ref, out_ref, sums_ref):
        lane = lax.broadcasted_iota(jnp.int32, (ROWS, 128), 1)
        for pair in range(heads // 2):
            at = pair * 128
            queries = qkv_ref[:, at : at + 128]
            keys = qkv_ref[:, width + at : width + at + 128]
            values = qkv_ref[:, 2 * width + at : 2 * width + at + 128]
            grad = grad_ref[:, at : at + 128]
            keys_t = (keys * BF16(0.125)).T
            queries_s = queries * BF16(0.125)
            d_query, d_key, d_value = [], [], []
            for half in range(2):
                inside = (lane < HEAD) if half == 0 else (lane >= HEAD)
                own_values = jnp.where(inside, values, jnp.zeros_like(values))
                low_probs = probs_ref[0, 2 * pair + half]
                prob_grad = dot(own_values, grad, NT)
                wide_probs = low_probs.astype(F32)
                product = prob_grad * wide_probs
                weighted = jnp.sum(product, axis=0, keepdims=True)
                score_grad = (product - wide_probs * weighted).astype(BF16)
                d_value.append(dot(low_probs, grad))
                d_key.append(dot(score_grad, queries_s))
                d_query.append(dot(keys_t[half * HEAD : (half + 1) * HEAD], score_grad))
            parts = [
                jnp.concatenate(d_query, 0).T,
                jnp.where(lane < HEAD, d_key[0], d_key[1]),
                jnp.where(lane < HEAD, d_value[0], d_value[1]),
            ]
            for n, part in enumerate(parts):
                out_ref[:, n * width + at : n * width + at + 128] = part.astype(BF16)
        total = jnp.sum(out_ref[...].astype(F32), axis=0, keepdims=True)
        total = jnp.broadcast_to(total, sums_ref.shape)

        @pl.when(pl.program_id(0) == 0)
        def _():
            sums_ref[...] = total

        @pl.when(pl.program_id(0) != 0)
        def _():
            sums_ref[...] += total

    return pl.pallas_call(
        kernel,
        grid=(2,),
        in_specs=[
            pl.BlockSpec(*image(3 * width)),
            pl.BlockSpec((1, heads, ROWS, ROWS), lambda i: (i, 0, 0, 0)),
            pl.BlockSpec(*image(width)),
        ],
        out_specs=[pl.BlockSpec(*image(3 * width)), pl.BlockSpec(*fixed(8, 3 * width))],
        out_shape=[
            jax.ShapeDtypeStruct((2 * ROWS, 3 * width), BF16),
            jax.ShapeDtypeStruct((8, 3 * width), F32),
        ],
        compiler_params=pltpu.CompilerParams(vmem_limit_bytes=VMEM_LIMIT),
        cost_estimate=LITTLE,
    )(projected, probs, mixed_grad)


def norm_two(tokens, low, moved, vectors):
    width = tokens.shape[1]

    def kernel(tokens_ref, low_ref, moved_ref, vec_ref, resid_ref, out_ref):
        branch = low_ref[...].astype(F32) + moved_ref[...].astype(F32)
        residual = tokens_ref[...].astype(F32) + branch + vec_ref[4:5]
        resid_ref[...] = residual
        hat, _ = row_stats(residual)
        out_ref[...] = (hat * vec_ref[2:3] + vec_ref[3:4]).astype(BF16)

    return call(
        kernel,
        (2,),
        [image(width), image(width), other_image(width), fixed(8, width)],
        [image(width) + (tokens.shape, F32), image(width) + (tokens.shape, BF16)],
        tokens,
        low,
        moved,
        vectors,
    )


def weight_grad(rows, grad):
    return rows_first(dot(rows, grad, TN).astype(BF16))


def attention_weight_grad(normed, qkv_grad, attn_grad, mixed):
    deep, width = normed.shape[1], mixed.shape[1]
    cut = 256
    half = 2 * width

    def kernel(normed_ref, qkv_ref, grad_ref, mixed_ref, first_ref, second_ref):
        grad = dot(normed_ref[...], qkv_ref[...], TN).astype(BF16)
        first_ref[...] = grad[:, :half]
        second_ref[:, :width] = grad[:, half:]
        second_ref[:, width:] = dot(grad_ref[...], mixed_ref[...], TN).astype(BF16)

    column = ((2 * ROWS, cut), lambda j: (0, j))
    out = ((cut, half), lambda j: (j, 0), (deep, half), BF16)
    return call(
        kernel,
        (deep // cut,),
        [column, fixed(2 * ROWS, 3 * width), column, fixed(2 * ROWS, width)],
        [out, out],
        normed,
        qkv_grad,
        attn_grad,
        mixed,
    )


def norm_two_back(low, moved, residual, down, vectors):
    width = low.shape[1]

    def kernel(low_ref, moved_ref, resid_ref, down_ref, vec_ref, own_ref, out_ref, sums_ref):
        back = low_ref[...].astype(F32) + moved_ref[...].astype(F32)
        upstream = down_ref[...].astype(F32)
        hat, inv = row_stats(resid_ref[...])
        grad = upstream + norm_back(back, hat, inv, vec_ref[2:3])
        out_ref[...] = grad.astype(BF16)

        @pl.when(pl.program_id(0) == 0)
        def _():
            own_ref[...] = grad
            for n, part in enumerate((back * hat, back, grad, upstream)):
                sums_ref[n : n + 1] = jnp.sum(part, axis=0, keepdims=True)

    return call(
        kernel,
        (2,),
        [image(width), other_image(width), image(width), image(width), fixed(8, width)],
        [
            fixed(ROWS, width) + ((ROWS, width), F32),
            image(width) + ((2 * ROWS, width), BF16),
            fixed(8, width) + ((8, width), F32),
        ],
        low,
        moved,
        residual,
        down,
        vectors,
    )


def norm_one_back(low, moved, tokens, grad, vectors):
    width = low.shape[1]

    def kernel(low_ref, moved_ref, tokens_ref, grad_ref, vec_ref, out_ref, sums_ref):
        back = low_ref[...].astype(F32) + moved_ref[...].astype(F32)
        hat, inv = row_stats(tokens_ref[...].astype(F32))
        total = grad_ref[...] + norm_back(back, hat, inv, vec_ref[0:1])
        out_ref[...] = total[:SEQ]
        for n, part in enumerate((back * hat, back)):
            sums_ref[n : n + 1] = jnp.sum(part, axis=0, keepdims=True)

    own_rows = fixed(ROWS, width)
    return call(
        kernel,
        (1,),
        [own_rows, own_rows, own_rows, own_rows, fixed(8, width)],
        [
            fixed(SEQ, width) + ((SEQ, width), F32),
            fixed(8, width) + ((8, width), F32),
        ],
        low,
        moved,
        tokens,
        grad,
        vectors,
    )


def layer_output(residual, low, moved, vectors):
    width = low.shape[1]

    def kernel(resid_ref, low_ref, moved_ref, vec_ref, out_ref):
        branch = low_ref[...].astype(F32) + moved_ref[...].astype(F32)
        out_ref[...] = (resid_ref[...] + branch + vec_ref[5:6]).astype(BF16)[:SEQ]

    own_rows = fixed(ROWS, width)
    out = fixed(SEQ, width) + ((SEQ, width), BF16)
    ins = [own_rows, own_rows, own_rows, fixed(8, width)]
    return call(kernel, (1,), ins, [out], residual, low, moved, vectors)[0]


def place(parts, spots, shape, block):
    def kernel(spot_ref, *refs):
        out_ref, sems = refs[-2], refs[-1]
        copies = []
        for n in range(len(parts)):
            copies.append(
                pltpu.make_async_copy(refs[n], block(out_ref, spot_ref[n]), sems.at[n])
            )
        for copy in copies:
            copy.start()
        for copy in copies:
            copy.wait()

    return pl.pallas_call(
        kernel,
        grid_spec=pltpu.PrefetchScalarGridSpec(
            num_scalar_prefetch=1,
            grid=(1,),
            in_specs=[pl.BlockSpec(memory_space=pl.ANY)] * len(parts),
            out_specs=pl.BlockSpec(memory_space=pl.ANY),
            scratch_shapes=[pltpu.SemaphoreType.DMA((len(parts),))],
        ),
        out_shape=jax.ShapeDtypeStruct(shape, parts[0].dtype),
        compiler_params=pltpu.CompilerParams(vmem_limit_bytes=2**20),
        cost_estimate=LITTLE,
    )(spots, *parts)


def pack(qkv, proj, quarter):
    def kernel(qkv_ref, proj_ref, out_ref):
        for colour in range(2):
            cut = slice(colour * quarter, (colour + 1) * quarter)
            for n in range(4):
                at = (4 * colour + n) * quarter
                part = qkv_ref[n, :, cut] if n < 3 else proj_ref[:, cut]
                out_ref[:, at : at + quarter] = part

    return pl.pallas_call(
        kernel,
        out_shape=jax.ShapeDtypeStruct((proj.shape[0], 8 * quarter), proj.dtype),
        compiler_params=pltpu.CompilerParams(vmem_limit_bytes=VMEM_LIMIT),
        cost_estimate=LITTLE,
    )(qkv, proj)


def build(n_z, n_x):
    sizes = dict(z=n_z, x=n_x, c=2, y=2)

    def pairs(move, only=None):
        found = []
        names = ALL
        spots = list(itertools.product(*[range(sizes[a]) for a in names]))
        index = {spot: n for n, spot in enumerate(spots)}
        for spot in spots:
            here = dict(zip(names, spot))
            if only is not None and not only(here):
                continue
            there = dict(here)
            move(there)
            found.append((index[spot], index[tuple(there[a] for a in names)]))
        return found

    def shift(axis, by, only=None):
        def move(spot):
            spot[axis] = (spot[axis] + by) % sizes[axis]

        return pairs(move, only)

    def flip(axis, by):
        def move(spot):
            spot[axis] ^= by

        return pairs(move)

    def send(value, perm):
        return lax.ppermute(value, ALL, perm)

    def exchange(spot):
        spot["c"], spot["y"] = spot["y"], spot["c"]

    transpose = pairs(exchange)

    def on_device(
        tokens,
        ln1_gain,
        ln1_bias,
        qkv_weight,
        qv_bias,
        proj_weight,
        proj_bias,
        ln2_gain,
        ln2_bias,
        fc1_weight,
        fc1_bias,
        fc2_weight,
        fc2_bias,
        cotangent,
    ):
        z, x, c, y = [lax.axis_index(a) for a in ALL]
        owner = c == y
        where_am_i = dict(z=z, x=x, c=c, y=y)
        width = tokens.shape[1]
        depth = fc1_weight.shape[0]
        heads = qv_bias.shape[1] // 2

        def swap(value):
            return send(value, shift("c", 1))

        def after(value, *earlier):
            return lax.optimization_barrier((value,) + earlier)[0]

        quarter = proj_weight.shape[0] // 2
        n_qkv = 3 * quarter
        hidden_half = fc1_weight.shape[1] // 2
        proj_t = proj_weight.T
        fc2_t = fc2_weight.T
        shards = [pack(qkv_weight.transpose(1, 0, 2), proj_t, quarter), fc1_weight, fc2_t]

        def spots(axis):
            count = sizes[axis]
            return (where_am_i[axis] + jnp.arange(count, dtype=jnp.int32)) % count

        def from_all(value, axis, shape, block, earlier=()):
            moved = [send(value, shift(axis, -k)) for k in range(1, sizes[axis])]
            if earlier:
                moved = [after(part, *earlier) for part in moved]
            return place([value] + moved, spots(axis), shape, block)

        def crossed(shard):
            return send(shard, transpose)

        def together(*values):
            return lax.optimization_barrier(values)

        def halves(line, *earlier):
            wide = line.shape[2] // 2
            return together(line[:, :, :wide], line[:, :, wide:], *earlier)[:2]

        def step_one(first, second, *earlier):
            at = (n_z, n_x, depth, first.shape[2])
            first = from_all(first, "x", at, lambda ref, n: ref.at[:, n], earlier)
            at = (n_z, 2, depth, second.shape[2])
            second = from_all(second, "y", at, lambda ref, n: ref.at[:, n], earlier)
            return together(first, second)

        def step_two(first, second, *earlier):
            wide = first.shape[3]
            at = (n_z, n_x, 2, depth, wide)
            first = from_all(first, "y", at, lambda ref, n: ref.at[:, :, n], earlier)
            second = from_all(second, "x", at, lambda ref, n: ref.at[:, n], earlier)
            return first.reshape(width, wide), second.reshape(width, wide)

        def pick(array, axis, index):
            return lax.dynamic_index_in_dim(array, index, axis, keepdims=False)

        def give(array, axis, dim):
            count, here = sizes[axis], where_am_i[axis]
            moved = [
                send(pick(array, dim, (here + k) % count), shift(axis, k))
                for k in range(1, count)
            ]
            return moved, pick(array, dim, here)

        def summed(given, *earlier):
            moved, own_part = given
            total = own_part.astype(F32)
            for part in moved:
                total = total + (after(part, *earlier) if earlier else part).astype(F32)
            return total.astype(BF16)

        def scatter_one(first, second):
            at = (n_z, n_x, 2, depth, first.shape[1])
            return give(first.reshape(at), "y", 2), give(second.reshape(at), "x", 1)

        def scatter_two(first, second):
            return give(first, "x", 1), give(second, "y", 1)

        def gathered(parts):
            return jnp.concatenate(parts, axis=2)

        def scatter_three(both):
            return lax.psum_scatter(both, "z", scatter_dimension=0, tiled=False)

        shard_one = crossed(shards[0])
        shard_two = crossed(after(shards[1], shard_one))
        shard_three = crossed(after(shards[2], shard_one))
        shard_one = after(shard_one, shard_two, shard_three)
        wide = shards[0].shape[1] // 2
        around = [shard_one] + [send(shard_one, shift("z", -k)) for k in range(1, n_z)]
        line_one = [
            place(
                [part[:, cut] for part in around],
                spots("z"),
                (n_z, depth, wide),
                lambda ref, n: ref.at[n],
            )
            for cut in (slice(0, wide), slice(wide, 2 * wide))
        ]
        line_one = together(*line_one)

        def both_images(value):
            value = jnp.pad(value, ((0, ROWS - SEQ), (0, 0)))
            return jnp.concatenate([value, swap(value)])

        inputs = both_images(after(tokens, around[1]))
        down = both_images(after(cotangent, around[1]))

        small = jnp.concatenate(
            [after(ln1_gain, around[1]), ln1_bias, ln2_gain, ln2_bias, proj_bias, fc2_bias]
            + [qv_bias.reshape(-1), fc1_bias.reshape(-1)]
        )[None]

        def spread(small, axis):
            for n in range(sizes[axis].bit_length() - 1):
                moved = send(small, flip(axis, 2**n))
                low_side = (where_am_i[axis] // 2**n) % 2 == 0
                small = jnp.where(
                    low_side, jnp.concatenate([small, moved]), jnp.concatenate([moved, small])
                )
            return small[None]

        for axis in ("c", "y", "x"):
            small = spread(small, axis)
        small = spread(after(small, *line_one), "z")
        square_one = step_one(*line_one, small)
        line_two = lax.all_gather(after(shard_two, small), "z", axis=0)
        line_three = lax.all_gather(after(shard_three, small), "z", axis=0)
        share = ln1_gain.shape[0]
        small = small.reshape(n_z, n_x, 2, 2, -1)
        small = small.transpose(0, 1, 3, 2, 4)
        vectors = small[..., : 6 * share].reshape(-1, 6, share).transpose(1, 0, 2).reshape(6, -1)
        vectors = jnp.pad(vectors.astype(F32), ((0, 2), (0, 0)))
        mine = pick(small[..., 6 * share :], 3, c).astype(F32)
        per_qv = qv_bias.shape[2]
        n_qv = qv_bias.size
        qv_half = mine[..., :n_qv].reshape((-1,) + qv_bias.shape)
        qv_half = qv_half.transpose(1, 2, 0, 3).reshape(2, -1)
        per_fc1 = fc1_bias.shape[1]
        fc1_half = mine[..., n_qv:].reshape((-1,) + fc1_bias.shape)
        fc1_half = fc1_half.transpose(1, 0, 2).reshape(-1)

        normed_one = norm_one(inputs, vectors)

        half_two = halves(line_two, normed_one)
        attn_w = step_two(*square_one, *half_two)
        projected, probs, mixed = [None] * 2, [None] * 2, [None] * 2

        def attend_half(colour, rows):
            cut = slice(colour * quarter, (colour + 1) * quarter)
            bias = jnp.concatenate(
                [qv_half[0, cut], jnp.zeros((quarter,), F32), qv_half[1, cut]]
            )
            projected[colour] = (dot(rows, attn_w[colour][:, :n_qkv]) + bias).astype(BF16)
            mixed[colour], probs[colour] = attend(projected[colour], heads)

        def back_product(lefts, weights):
            return (dot(lefts[0], weights[0], NT) + dot(lefts[1], weights[1], NT)).astype(BF16)

        attend_half(0, normed_one)
        square_two = step_one(*half_two, mixed[0])
        attend_half(1, after(normed_one, *square_two))
        half_three = halves(line_three, mixed[1])
        fc1_w = step_two(*square_two, *half_three)
        proj_ab = [w[:, n_qkv:] for w in attn_w]
        low = back_product([after(m, *fc1_w) for m in mixed], proj_ab)
        residual, normed_two = norm_two(inputs, low, swap(low), vectors)
        square_three = step_one(*half_three, normed_two)

        hidden, slope = [], []
        rows_two = after(normed_two, *square_three)
        for colour, weight in enumerate(fc1_w):
            bias = fc1_half[colour * hidden_half : (colour + 1) * hidden_half]
            pre = dot(rows_two, weight) + bias
            cdf = 0.5 * (1.0 + lax.erf(pre * (1.0 / math.sqrt(2.0))))
            density = jnp.exp(-0.5 * pre * pre) * (1.0 / math.sqrt(2.0 * math.pi))
            hidden.append((pre * cdf).astype(BF16))
            slope.append((cdf + pre * density).astype(BF16))

        grad_fc2 = [weight_grad(down, h) for h in hidden]
        fc2_one = scatter_one(*grad_fc2)
        fc2_w = step_two(*square_three, *grad_fc2)
        down_late = after(down, *fc2_w)
        hidden_grad = [
            (dot(down_late, w) * s.astype(F32)).astype(BF16) for w, s in zip(fc2_w, slope)
        ]
        unit_sums = [jnp.sum(g.astype(F32), axis=0) for g in hidden_grad]
        low = back_product(hidden_grad, fc1_w)
        moved = swap(low)
        fc2_sums = [summed(given, low) for given in fc2_one]
        fc2_two = scatter_two(*fc2_sums)
        normed_late = after(normed_two, *fc2_sums)
        grad_fc1 = [weight_grad(normed_late, g) for g in hidden_grad]
        fc1_one = scatter_one(*grad_fc1)
        resid_grad, attn_grad, sums_two = norm_two_back(
            low, after(moved, *grad_fc1), residual, down, vectors
        )

        fc2_lines = gathered([summed(given, attn_grad) for given in fc2_two])
        scat_fc2 = scatter_three(fc2_lines)
        attn_late = after(attn_grad, fc2_lines)
        mixed_grad = [dot(attn_late, w).astype(BF16) for w in proj_ab]
        back_a, sums_a = attend_back(projected[0], probs[0], mixed_grad[0], heads)
        grads_a = attention_weight_grad(normed_one, back_a, attn_grad, mixed[0])
        a_one = scatter_one(*grads_a)
        fc1_sums = [summed(given, *grads_a) for given in fc1_one]
        fc1_two = scatter_two(*fc1_sums)
        back_b, sums_b = attend_back(
            after(projected[1], *fc1_sums), probs[1], mixed_grad[1], heads
        )
        fc1_lines = gathered([summed(given, back_b) for given in fc1_two])
        scat_fc1 = scatter_three(fc1_lines)
        a_sums = [summed(given, fc1_lines) for given in a_one]
        a_two = scatter_two(*a_sums)
        grads_b = attention_weight_grad(
            after(normed_one, *a_sums, scat_fc2), back_b, attn_grad, mixed[1]
        )
        b_one = scatter_one(*grads_b)
        a_lines = gathered([summed(given, *grads_b) for given in a_two])
        scat_a = scatter_three(a_lines)
        qkv_ab = [w[:, :n_qkv] for w in attn_w]
        low = back_product((after(back_a, a_lines), back_b), qkv_ab)
        b_sums = [summed(given, low) for given in b_one]
        b_two = scatter_two(*b_sums)
        moved = after(swap(low[ROWS:]), *b_sums, scat_fc1)
        grad_tokens, sums_one = norm_one_back(low, moved, inputs, resid_grad, vectors)
        b_lines = gathered([summed(given, grad_tokens) for given in b_two])
        scat_b = scatter_three(b_lines)
        scat_attn = jnp.concatenate([scat_a, scat_b], axis=1)
        scat_fc1, scat_fc2, scat_attn = [
            send(part, transpose) for part in (scat_fc1, scat_fc2, scat_attn)
        ]
        scat_attn = scat_attn.astype(F32)

        hidden_late = [after(h, b_lines, scat_a) for h in hidden]
        branch_two = back_product(hidden_late, fc2_w)
        output = layer_output(residual, branch_two, swap(branch_two[ROWS:]), vectors)

        six = [sums_one[0], sums_one[1]] + [sums_two[n] for n in range(4)]
        grad_qv = [sums_a[0], sums_b[0]]
        grad_fc1_shift = jnp.concatenate(unit_sums)
        halves = [g[:quarter] for g in grad_qv] + [g[2 * quarter :] for g in grad_qv]
        sums = jnp.concatenate(six + halves + [grad_fc1_shift])[None]
        for axis in ("z", "x", "y"):
            moved = [send(sums, shift(axis, k)) for k in range(1, sizes[axis])]
            sums = functools.reduce(jnp.add, moved, sums)
        moved = swap(sums)[0]
        sums = sums[0]
        spot = ((z * n_x + x) * 2 + c) * 2 + y
        small_own = (sums[: 6 * width] + moved[: 6 * width]).reshape(6, -1, share)
        small_own = pick(small_own, 1, spot)
        half = jnp.where(owner, sums[6 * width :], moved[6 * width :])
        deep = (z * n_x + x) * 2 + c
        grad_qv = half[: 4 * quarter].reshape(2, qv_bias.shape[1], -1, per_qv)
        grad_qv = pick(grad_qv, 2, deep)
        grad_fc1_bias = pick(half[4 * quarter :].reshape(fc1_bias.shape[0], -1, per_fc1), 1, deep)

        def joined(index):
            at = index * quarter
            cuts = [scat_attn[:, at + half : at + half + quarter] for half in (0, 4 * quarter)]
            return jnp.concatenate(cuts, axis=1)

        grad_qkv = jnp.stack([joined(0), joined(1), joined(2)], axis=1)
        return (
            output,
            grad_tokens,
            small_own[0],
            small_own[1],
            grad_qkv,
            grad_qv,
            joined(3).T,
            small_own[4],
            small_own[2],
            small_own[3],
            scat_fc1.astype(F32),
            grad_fc1_bias,
            scat_fc2.astype(F32).T,
            small_own[5],
        )

    return on_device


def solution(mesh):
    chips = mesh.shape["dp"] // 2
    n_x = 1
    while n_x * n_x * 4 <= chips and chips % (n_x * 2) == 0:
        n_x *= 2
    n_z = chips // n_x
    fine = Mesh(np.asarray(mesh.devices).reshape(n_z, n_x, 2, 2), ALL)
    dp = ("z", "x", "c")
    every = P(ALL)
    rows = P(ALL, None)
    in_specs = (
        rows,
        every,
        every,
        P(dp, None, "y"),
        P(None, "y", dp),
        P("y", dp),
        every,
        every,
        every,
        P(dp, "y"),
        P("y", dp),
        P("y", dp),
        every,
        rows,
    )
    out_specs = (
        rows,
        rows,
        every,
        every,
        P(dp, None, "y"),
        P(None, "y", dp),
        P("y", dp),
        every,
        every,
        every,
        P(dp, "y"),
        P("y", dp),
        P("y", dp),
        every,
    )
    return jax.shard_map(
        build(n_z, n_x), mesh=fine, in_specs=in_specs, out_specs=out_specs, check_vma=False
    )
```

```python
import functools
import itertools
import math

import jax
import jax.numpy as jnp
import numpy as np
from jax import lax
from jax.experimental import pallas as pl
from jax.experimental.pallas import tpu as pltpu
from jax.experimental.layout import Layout, with_layout_constraint
from jax.sharding import Mesh
from jax.sharding import PartitionSpec as P

SEQ = 577
ROWS = 592
HEAD = 64
EPS = 1e-06
ALL = ("z", "x", "c", "y")
F32 = jnp.float32
BF16 = jnp.bfloat16

NN = (((1,), (0,)), ((), ()))
NT = (((1,), (1,)), ((), ()))
TN = (((0,), (0,)), ((), ()))
VMEM_LIMIT = 20 * 2**20
LITTLE = pl.CostEstimate(flops=2**20, bytes_accessed=2**18, transcendentals=0)


def rows_first(array):
    return with_layout_constraint(array, Layout(major_to_minor=(0, 1)))


def dot(left, right, dims=NN):
    return lax.dot_general(left, right, dims, preferred_element_type=F32)


def call(kernel, grid, ins, outs, *arrays):
    return pl.pallas_call(
        kernel,
        grid=grid,
        in_specs=[pl.BlockSpec(block, at) for block, at in ins],
        out_specs=[pl.BlockSpec(block, at) for block, at, _, _ in outs],
        out_shape=[jax.ShapeDtypeStruct(shape, dtype) for _, _, shape, dtype in outs],
        compiler_params=pltpu.CompilerParams(vmem_limit_bytes=VMEM_LIMIT),
        cost_estimate=LITTLE,
    )(*arrays)


def image(width):
    return (ROWS, width), lambda i: (i, 0)


def other_image(width):
    return (ROWS, width), lambda i: (1 - i, 0)


def fixed(*block):
    return block, lambda *i: (0,) * len(block)


def row_stats(values):
    mean = jnp.mean(values, axis=-1, keepdims=True)
    centered = values - mean
    inv = lax.rsqrt(jnp.mean(jnp.square(centered), axis=-1, keepdims=True) + EPS)
    return centered * inv, inv


def norm_back(upstream, normed, inv_scale, gain):
    scaled = upstream * gain
    first = jnp.mean(scaled, axis=-1, keepdims=True)
    second = jnp.mean(scaled * normed, axis=-1, keepdims=True)
    return inv_scale * (scaled - first - normed * second)


def norm_one(tokens, vectors):
    width = tokens.shape[1]

    def kernel(tokens_ref, vec_ref, out_ref):
        hat, _ = row_stats(tokens_ref[...].astype(F32))
        out_ref[...] = (hat * vec_ref[0:1] + vec_ref[1:2]).astype(BF16)

    out = image(width) + (tokens.shape, BF16)
    return call(kernel, (2,), [image(width), fixed(8, width)], [out], tokens, vectors)[0]


def attend(projected, heads):
    width = heads * HEAD

    def kernel(qkv_ref, mixed_ref, probs_ref):
        lane = lax.broadcasted_iota(jnp.int32, (ROWS, 128), 1)
        row = lax.broadcasted_iota(jnp.int32, (ROWS, ROWS), 0)
        for pair in range(heads // 2):
            at = pair * 128
            queries = qkv_ref[:, at : at + 128]
            keys = qkv_ref[:, width + at : width + at + 128]
            values = qkv_ref[:, 2 * width + at : 2 * width + at + 128]
            mixed = []
            for half in range(2):
                inside = (lane < HEAD) if half == 0 else (lane >= HEAD)
                own_keys = jnp.where(inside, keys, jnp.zeros_like(keys)) * BF16(0.125)
                scores = dot(own_keys, queries, NT)
                scores = jnp.where(row < SEQ, scores, -1e30)
                shifted = jnp.exp(scores - jnp.max(scores, axis=0, keepdims=True))
                total = jnp.sum(shifted, axis=0, keepdims=True)
                probs = (shifted * (1.0 / total)).astype(BF16)
                probs_ref[0, 2 * pair + half] = probs
                mixed.append(dot(probs, values, TN))
            mixed_ref[:, at : at + 128] = jnp.where(lane < HEAD, mixed[0], mixed[1]).astype(BF16)

    rows = 2 * ROWS
    return call(
        kernel,
        (2,),
        [image(3 * width)],
        [
            image(width) + ((rows, width), BF16),
            ((1, heads, ROWS, ROWS), lambda i: (i, 0, 0, 0), (2, heads, ROWS, ROWS), BF16),
        ],
        projected,
    )


def attend_back(projected, probs, attn_grad, weight, heads):
    width = heads * HEAD
    deep = attn_grad.shape[1]

    def kernel(qkv_ref, probs_ref, grad_ref, weight_ref, out_ref, sums_ref, mixed_ref):
        mixed_ref[...] = dot(grad_ref[...], weight_ref[...]).astype(BF16)
        lane = lax.broadcasted_iota(jnp.int32, (ROWS, 128), 1)
        for pair in range(heads // 2):
            at = pair * 128
            queries = qkv_ref[:, at : at + 128]
            keys = qkv_ref[:, width + at : width + at + 128]
            values = qkv_ref[:, 2 * width + at : 2 * width + at + 128]
            grad = mixed_ref[:, at : at + 128]
            keys_t = (keys * BF16(0.125)).T
            queries_s = queries * BF16(0.125)
            d_query, d_key, d_value = [], [], []
            for half in range(2):
                inside = (lane < HEAD) if half == 0 else (lane >= HEAD)
                own_values = jnp.where(inside, values, jnp.zeros_like(values))
                low_probs = probs_ref[0, 2 * pair + half]
                prob_grad = dot(own_values, grad, NT)
                wide_probs = low_probs.astype(F32)
                product = prob_grad * wide_probs
                weighted = jnp.sum(product, axis=0, keepdims=True)
                score_grad = (product - wide_probs * weighted).astype(BF16)
                d_value.append(dot(low_probs, grad))
                d_key.append(dot(score_grad, queries_s))
                d_query.append(dot(keys_t[half * HEAD : (half + 1) * HEAD], score_grad))
            parts = [
                jnp.concatenate(d_query, 0).T,
                jnp.where(lane < HEAD, d_key[0], d_key[1]),
                jnp.where(lane < HEAD, d_value[0], d_value[1]),
            ]
            for n, part in enumerate(parts):
                out_ref[:, n * width + at : n * width + at + 128] = part.astype(BF16)
        total = jnp.sum(out_ref[...].astype(F32), axis=0, keepdims=True)
        total = jnp.broadcast_to(total, sums_ref.shape)

        @pl.when(pl.program_id(0) == 0)
        def _():
            sums_ref[...] = total

        @pl.when(pl.program_id(0) != 0)
        def _():
            sums_ref[...] += total

    return pl.pallas_call(
        kernel,
        grid=(2,),
        in_specs=[
            pl.BlockSpec(*image(3 * width)),
            pl.BlockSpec((1, heads, ROWS, ROWS), lambda i: (i, 0, 0, 0)),
            pl.BlockSpec(*image(deep)),
            pl.BlockSpec((deep, width), lambda i: (0, 3)),
        ],
        out_specs=[pl.BlockSpec(*image(3 * width)), pl.BlockSpec(*fixed(8, 3 * width))],
        out_shape=[
            jax.ShapeDtypeStruct((2 * ROWS, 3 * width), BF16),
            jax.ShapeDtypeStruct((8, 3 * width), F32),
        ],
        scratch_shapes=[pltpu.VMEM((ROWS, width), BF16)],
        compiler_params=pltpu.CompilerParams(vmem_limit_bytes=VMEM_LIMIT),
        cost_estimate=LITTLE,
    )(projected, probs, attn_grad, weight)


def pieces(width):
    unit = width // 128
    part = -(-unit // 3) * 128
    return [part, part, width - 2 * part]


def joined_columns(refs):
    return jnp.concatenate([ref[...] for ref in refs], axis=1).astype(F32)


def rows_product(lefts, weights, block, split):
    width = lefts[0].shape[1]
    deep = weights[0].shape[0]
    count = len(lefts)
    cuts = pieces(deep)

    def kernel(*refs):
        outs = refs[2 * count :]
        total = dot(refs[0][...], refs[count][...], NT)
        for n in range(1, count):
            total = total + dot(refs[n][...], refs[count + n][...], NT)
        total = total.astype(BF16)

        def put(refs_out):
            at = 0
            for ref, cut in zip(refs_out, cuts):
                ref[...] = total[:, at : at + cut]
                at += cut

        if not split:
            put(outs)
            return

        @pl.when(pl.program_id(0) == 0)
        def _():
            outs[0][...] = total

        @pl.when(pl.program_id(0) != 0)
        def _():
            put(outs[1:])

    if split:
        outs = [fixed(ROWS, deep) + ((ROWS, deep), BF16)]
        outs += [fixed(ROWS, cut) + ((ROWS, cut), BF16) for cut in cuts]
    else:
        outs = [image(cut) + ((2 * ROWS, cut), BF16) for cut in cuts]
    ins = [image(width)] * count + [block] * count
    found = call(kernel, (2,), ins, outs, *lefts, *weights)
    return (found[0], found[1:]) if split else found


def norm_two(tokens, low, moved, vectors):
    width = tokens.shape[1]
    count = len(low)

    def kernel(tokens_ref, vec_ref, *refs):
        resid_ref, out_ref = refs[2 * count :]
        branch = joined_columns(refs[:count]) + joined_columns(refs[count : 2 * count])
        residual = tokens_ref[...].astype(F32) + branch + vec_ref[4:5]
        resid_ref[...] = residual
        hat, _ = row_stats(residual)
        out_ref[...] = (hat * vec_ref[2:3] + vec_ref[3:4]).astype(BF16)

    ins = [image(width), fixed(8, width)]
    ins += [image(part.shape[1]) for part in low] + [other_image(part.shape[1]) for part in moved]
    outs = [image(width) + (tokens.shape, F32), image(width) + (tokens.shape, BF16)]
    return call(kernel, (2,), ins, outs, tokens, vectors, *low, *moved)


def hidden_units(normed, weight, bias):
    deep, width = weight.shape
    cut = 512

    def kernel(rows_ref, weight_ref, bias_ref, hidden_ref, slope_ref):
        pre = dot(rows_ref[...], weight_ref[...]) + bias_ref[0:1]
        cdf = 0.5 * (1.0 + lax.erf(pre * (1.0 / math.sqrt(2.0))))
        density = jnp.exp(-0.5 * pre * pre) * (1.0 / math.sqrt(2.0 * math.pi))
        hidden_ref[...] = (pre * cdf).astype(BF16)
        slope_ref[...] = (cdf + pre * density).astype(BF16)

    out = ((ROWS, cut), lambda j, i: (i, j), (2 * ROWS, width), BF16)
    return call(
        kernel,
        (width // cut, 2),
        [
            ((ROWS, deep), lambda j, i: (i, 0)),
            ((deep, cut), lambda j, i: (0, j)),
            ((8, cut), lambda j, i: (0, j)),
        ],
        [out, out],
        normed,
        weight,
        bias,
    )


def hidden_back(down, weight, slope):
    deep, width = weight.shape
    cut = 1024

    def kernel(rows_ref, weight_ref, slope_ref, out_ref, sums_ref):
        grad = (dot(rows_ref[...], weight_ref[...]) * slope_ref[...].astype(F32)).astype(BF16)
        out_ref[...] = grad
        total = jnp.sum(grad.astype(F32), axis=0, keepdims=True)
        total = jnp.broadcast_to(total, sums_ref.shape)

        @pl.when(pl.program_id(1) == 0)
        def _():
            sums_ref[...] = total

        @pl.when(pl.program_id(1) != 0)
        def _():
            sums_ref[...] += total

    return call(
        kernel,
        (width // cut, 2),
        [
            ((ROWS, deep), lambda j, i: (i, 0)),
            ((deep, cut), lambda j, i: (0, j)),
            ((ROWS, cut), lambda j, i: (i, j)),
        ],
        [
            ((ROWS, cut), lambda j, i: (i, j), (2 * ROWS, width), BF16),
            ((8, cut), lambda j, i: (0, j), (8, width), F32),
        ],
        down,
        weight,
        slope,
    )


def weight_grad_kernel(rows, grad):
    deep, width = rows.shape[1], grad.shape[1]
    cut = 256

    def kernel(rows_ref, grad_ref, out_ref):
        out_ref[...] = dot(rows_ref[...], grad_ref[...], TN).astype(BF16)

    return call(
        kernel,
        (deep // cut,),
        [((2 * ROWS, cut), lambda j: (0, j)), fixed(2 * ROWS, width)],
        [((cut, width), lambda j: (j, 0), (deep, width), BF16)],
        rows,
        grad,
    )[0]


def weight_grad(rows, grad):
    return rows_first(dot(rows, grad, TN).astype(BF16))


def attention_weight_grad(normed, qkv_grad, attn_grad, mixed):
    deep, width = normed.shape[1], mixed.shape[1]
    cut = 256
    half = 2 * width

    def kernel(normed_ref, qkv_ref, grad_ref, mixed_ref, first_ref, second_ref):
        grad = dot(normed_ref[...], qkv_ref[...], TN).astype(BF16)
        first_ref[...] = grad[:, :half]
        second_ref[:, :width] = grad[:, half:]
        second_ref[:, width:] = dot(grad_ref[...], mixed_ref[...], TN).astype(BF16)

    column = ((2 * ROWS, cut), lambda j: (0, j))
    out = ((cut, half), lambda j: (j, 0), (deep, half), BF16)
    return call(
        kernel,
        (deep // cut,),
        [column, fixed(2 * ROWS, 3 * width), column, fixed(2 * ROWS, width)],
        [out, out],
        normed,
        qkv_grad,
        attn_grad,
        mixed,
    )


def norm_two_back(low, moved, residual, down, vectors):
    width = residual.shape[1]
    count = len(low)

    def kernel(resid_ref, down_ref, vec_ref, *refs):
        own_ref, out_ref, sums_ref = refs[2 * count :]
        back = joined_columns(refs[:count]) + joined_columns(refs[count : 2 * count])
        upstream = down_ref[...].astype(F32)
        hat, inv = row_stats(resid_ref[...])
        grad = upstream + norm_back(back, hat, inv, vec_ref[2:3])
        out_ref[...] = grad.astype(BF16)

        @pl.when(pl.program_id(0) == 0)
        def _():
            own_ref[...] = grad
            for n, part in enumerate((back * hat, back, grad, upstream)):
                sums_ref[n : n + 1] = jnp.sum(part, axis=0, keepdims=True)

    ins = [image(width), image(width), fixed(8, width)]
    ins += [image(part.shape[1]) for part in low] + [other_image(part.shape[1]) for part in moved]
    outs = [
        fixed(ROWS, width) + ((ROWS, width), F32),
        image(width) + ((2 * ROWS, width), BF16),
        fixed(8, width) + ((8, width), F32),
    ]
    return call(kernel, (2,), ins, outs, residual, down, vectors, *low, *moved)


def norm_one_back(low, moved, tokens, grad, vectors):
    width = low.shape[1]
    count = len(moved)

    def kernel(low_ref, tokens_ref, grad_ref, vec_ref, *refs):
        out_ref, sums_ref = refs[count:]
        back = low_ref[...].astype(F32) + joined_columns(refs[:count])
        hat, inv = row_stats(tokens_ref[...].astype(F32))
        total = grad_ref[...] + norm_back(back, hat, inv, vec_ref[0:1])
        out_ref[...] = total[:SEQ]
        for n, part in enumerate((back * hat, back)):
            sums_ref[n : n + 1] = jnp.sum(part, axis=0, keepdims=True)

    own_rows = fixed(ROWS, width)
    ins = [own_rows, own_rows, own_rows, fixed(8, width)]
    ins += [fixed(ROWS, part.shape[1]) for part in moved]
    outs = [fixed(SEQ, width) + ((SEQ, width), F32), fixed(8, width) + ((8, width), F32)]
    return call(kernel, (1,), ins, outs, low, tokens, grad, vectors, *moved)


def layer_output(residual, low, moved, vectors):
    width = low.shape[1]

    def kernel(resid_ref, low_ref, vec_ref, *refs):
        branch = low_ref[...].astype(F32) + joined_columns(refs[:-1])
        refs[-1][...] = (resid_ref[...] + branch + vec_ref[5:6]).astype(BF16)[:SEQ]

    own_rows = fixed(ROWS, width)
    out = fixed(SEQ, width) + ((SEQ, width), BF16)
    ins = [own_rows, own_rows, fixed(8, width)] + [fixed(ROWS, p.shape[1]) for p in moved]
    return call(kernel, (1,), ins, [out], residual, low, vectors, *moved)[0]


def place(parts, spots, shape, dim):
    part = parts[0].shape
    block = shape[:dim] + (1,) + shape[dim + 1 :]
    before, later = (0,) * dim, (0,) * (len(shape) - dim - 1)

    def kernel(spot_ref, *refs):
        out_ref = refs[-1]
        for n in range(len(parts)):

            @pl.when(pl.program_id(0) == n)
            def _():
                out_ref[...] = refs[n][...].reshape(block)

    return pl.pallas_call(
        kernel,
        grid_spec=pltpu.PrefetchScalarGridSpec(
            num_scalar_prefetch=1,
            grid=(len(parts),),
            in_specs=[pl.BlockSpec(part, lambda i, spot: (0,) * len(part))] * len(parts),
            out_specs=pl.BlockSpec(block, lambda i, spot: before + (spot[i],) + later),
        ),
        out_shape=jax.ShapeDtypeStruct(shape, parts[0].dtype),
        compiler_params=pltpu.CompilerParams(vmem_limit_bytes=VMEM_LIMIT),
        cost_estimate=LITTLE,
    )(spots, *parts)


def at_index(parts, index):
    found = parts[0]
    for n in range(1, len(parts)):
        found = jnp.where(index == n, parts[n], found)
    return found


def prefetched(kernel, spots, steps, ins, outs, arrays):
    return pl.pallas_call(
        kernel,
        grid_spec=pltpu.PrefetchScalarGridSpec(
            num_scalar_prefetch=1,
            grid=(steps,),
            in_specs=[pl.BlockSpec(block, at) for block, at in ins],
            out_specs=[pl.BlockSpec(block, at) for block, at, _ in outs],
        ),
        out_shape=[jax.ShapeDtypeStruct(shape, BF16) for _, _, shape in outs],
        compiler_params=pltpu.CompilerParams(vmem_limit_bytes=VMEM_LIMIT),
        cost_estimate=LITTLE,
    )(spots, *arrays)


def parts_to_give(first, second, spots, wide, columns):
    n_z, n_x, _, depth, _ = first.shape
    at_a, at_b = columns

    def kernel(spot_ref, *refs):
        half = len(refs) // 2
        for n in range(half):
            refs[half + n][...] = refs[n][...].reshape(refs[half + n].shape)

    ins = [((1, n_x, 1, depth, wide), lambda i, s: (i, 0, s[1], 0, at_a))]
    outs = [((1, n_x, depth, wide), lambda i, s: (i, 0, 0, 0), (n_z, n_x, depth, wide))]
    for k in range(1, n_x):
        ins.append(((1, 1, 2, depth, wide), lambda i, s, k=k: (i, s[2 + k], 0, 0, at_b)))
        outs.append(((1, 2, depth, wide), lambda i, s: (i, 0, 0, 0), (n_z, 2, depth, wide)))
    arrays = [first] + [second] * (n_x - 1)
    found = prefetched(kernel, spots, n_z, ins, outs, arrays)
    return found[0], found[1:]


def sums_to_give(first, first_moved, second, second_moved, spots, wide, columns):
    n_z, n_x, _, depth, _ = first.shape
    at_a, at_b = columns

    def kernel(spot_ref, first_ref, moved_ref, second_ref, *refs):
        moved_refs, outs = refs[: n_x - 1], refs[n_x - 1 :]
        sums = []
        for x in range(n_x):
            total = first_ref[0, x, 0].astype(F32) + moved_ref[0, x].astype(F32)
            sums.append(total)
        for k in range(n_x):
            outs[k][0] = at_index(sums, spot_ref[2 + k]).astype(BF16)
        sums = []
        for y in range(2):
            total = second_ref[0, 0, y].astype(F32)
            for ref in moved_refs:
                total = total + ref[0, y].astype(F32)
            sums.append(total)
        for k in range(2):
            outs[n_x + k][0] = at_index(sums, spot_ref[k]).astype(BF16)

    ins = [
        ((1, n_x, 1, depth, wide), lambda i, s: (i, 0, s[0], 0, at_a)),
        ((1, n_x, depth, wide), lambda i, s: (i, 0, 0, 0)),
        ((1, 1, 2, depth, wide), lambda i, s: (i, s[2], 0, 0, at_b)),
    ] + [((1, 2, depth, wide), lambda i, s: (i, 0, 0, 0))] * (n_x - 1)
    out = ((1, depth, wide), lambda i, s: (i, 0, 0), (n_z, depth, wide))
    arrays = [first, first_moved, second, *second_moved]
    found = prefetched(kernel, spots, n_z, ins, [out] * (n_x + 2), arrays)
    return found[0], found[1:n_x], found[n_x], found[n_x + 1]


def line_sums(first, first_moved, second, second_moved):
    n_z, depth, wide = first.shape

    def kernel(first_ref, *refs):
        count = len(first_moved)
        second_ref, moved_ref, out_ref = refs[count:]
        total = first_ref[0].astype(F32)
        for ref in refs[:count]:
            total = total + ref[0].astype(F32)
        out_ref[0, :, :wide] = total.astype(BF16)
        total = second_ref[0].astype(F32) + moved_ref[0].astype(F32)
        out_ref[0, :, wide:] = total.astype(BF16)

    block = ((1, depth, wide), lambda i: (i, 0, 0))
    out = ((1, depth, 2 * wide), lambda i: (i, 0, 0), (n_z, depth, 2 * wide), BF16)
    arrays = [first, *first_moved, second, second_moved]
    return call(kernel, (n_z,), [block] * len(arrays), [out], *arrays)[0]


def pack(qkv, proj, quarter):
    def kernel(qkv_ref, proj_ref, out_ref):
        for colour in range(2):
            cut = slice(colour * quarter, (colour + 1) * quarter)
            for n in range(4):
                at = (4 * colour + n) * quarter
                part = qkv_ref[n, :, cut] if n < 3 else proj_ref[:, cut]
                out_ref[:, at : at + quarter] = part

    return pl.pallas_call(
        kernel,
        out_shape=jax.ShapeDtypeStruct((proj.shape[0], 8 * quarter), proj.dtype),
        compiler_params=pltpu.CompilerParams(vmem_limit_bytes=VMEM_LIMIT),
        cost_estimate=LITTLE,
    )(qkv, proj)


def build(n_z, n_x):
    sizes = dict(z=n_z, x=n_x, c=2, y=2)

    def pairs(move, only=None):
        found = []
        names = ALL
        spots = list(itertools.product(*[range(sizes[a]) for a in names]))
        index = {spot: n for n, spot in enumerate(spots)}
        for spot in spots:
            here = dict(zip(names, spot))
            if only is not None and not only(here):
                continue
            there = dict(here)
            move(there)
            found.append((index[spot], index[tuple(there[a] for a in names)]))
        return found

    def shift(axis, by, only=None):
        def move(spot):
            spot[axis] = (spot[axis] + by) % sizes[axis]

        return pairs(move, only)

    def flip(axis, by):
        def move(spot):
            spot[axis] ^= by

        return pairs(move)

    def send(value, perm):
        return lax.ppermute(value, ALL, perm)

    def exchange(spot):
        spot["c"], spot["y"] = spot["y"], spot["c"]

    transpose = pairs(exchange)

    def on_device(
        tokens,
        ln1_gain,
        ln1_bias,
        qkv_weight,
        qv_bias,
        proj_weight,
        proj_bias,
        ln2_gain,
        ln2_bias,
        fc1_weight,
        fc1_bias,
        fc2_weight,
        fc2_bias,
        cotangent,
    ):
        z, x, c, y = [lax.axis_index(a) for a in ALL]
        owner = c == y
        where_am_i = dict(z=z, x=x, c=c, y=y)
        width = tokens.shape[1]
        depth = fc1_weight.shape[0]
        heads = qv_bias.shape[1] // 2

        def swap(value):
            return send(value, shift("c", 1))

        def after(value, *earlier):
            return lax.optimization_barrier((value,) + earlier)[0]

        quarter = proj_weight.shape[0] // 2
        n_qkv = 3 * quarter
        hidden_half = fc1_weight.shape[1] // 2
        proj_t = proj_weight.T
        fc2_t = fc2_weight.T
        shards = [pack(qkv_weight.transpose(1, 0, 2), proj_t, quarter), fc1_weight, fc2_t]

        def spots(axis):
            count = sizes[axis]
            return (where_am_i[axis] + jnp.arange(count, dtype=jnp.int32)) % count

        def from_all(value, axis, shape, dim, earlier=()):
            moved = [send(value, shift(axis, -k)) for k in range(1, sizes[axis])]
            if earlier:
                moved = [after(part, *earlier) for part in moved]
            return place([value] + moved, spots(axis), shape, dim)

        def crossed(shard):
            return send(shard, transpose)

        def together(*values):
            return lax.optimization_barrier(values)

        def halves(line, *earlier):
            wide = line.shape[2] // 2
            return together(line[:, :, :wide], line[:, :, wide:], *earlier)[:2]

        def step_one(first, second, *earlier):
            at = (n_z, n_x, depth, first.shape[2])
            first = from_all(first, "x", at, 1, earlier)
            at = (n_z, 2, depth, second.shape[2])
            second = from_all(second, "y", at, 1, earlier)
            return together(first, second)

        def step_two(first, second, *earlier):
            wide = first.shape[3]
            at = (n_z, n_x, 2, depth, wide)
            first = from_all(first, "y", at, 2, earlier)
            second = from_all(second, "x", at, 1, earlier)
            return first.reshape(width, wide), second.reshape(width, wide)

        def pick(array, axis, index):
            return lax.dynamic_index_in_dim(array, index, axis, keepdims=False)

        grad_spots = jnp.concatenate([spots("y"), spots("x")])

        def scatter_one(first, second, columns=(0, 0)):
            at = (n_z, n_x, 2, depth, first.shape[1])
            first, second = first.reshape(at), second.reshape(at)
            parts = first.shape[4] // (max(columns) + 1)
            to_y, to_x = parts_to_give(first, second, grad_spots, parts, columns)
            from_y = send(to_y, shift("y", 1))
            from_x = [send(part, shift("x", k + 1)) for k, part in enumerate(to_x)]
            return (first, from_y, second, from_x, parts, columns), (to_y, *to_x)

        def scatter_two(given, *earlier):
            first, from_y, second, from_x, parts, columns = given
            if earlier:
                from_y, from_x = after(from_y, *earlier), [after(v, *earlier) for v in from_x]
            own_a, to_x, own_b, to_y = sums_to_give(
                first, from_y, second, from_x, grad_spots, parts, columns
            )
            from_x = [send(part, shift("x", k + 1)) for k, part in enumerate(to_x)]
            return own_a, from_x, own_b, send(to_y, shift("y", 1))

        def lines(given, *earlier):
            own_a, from_x, own_b, from_y = given
            from_y, from_x = after(from_y, *earlier), [after(v, *earlier) for v in from_x]
            return line_sums(own_a, from_x, own_b, from_y)

        def scatter_three(both):
            return lax.psum_scatter(both, "z", scatter_dimension=0, tiled=False)

        shard_one = crossed(shards[0])
        wide = shards[0].shape[1] // 2
        around = [shard_one] + [send(shard_one, shift("z", -k)) for k in range(1, n_z)]

        small = jnp.concatenate(
            [after(ln1_gain, shard_one), ln1_bias, ln2_gain, ln2_bias, proj_bias, fc2_bias]
            + [qv_bias.reshape(-1), fc1_bias.reshape(-1)]
        )[None]

        def spread(small, axis):
            for n in range(sizes[axis].bit_length() - 1):
                moved = send(small, flip(axis, 2**n))
                low_side = (where_am_i[axis] // 2**n) % 2 == 0
                small = jnp.where(
                    low_side, jnp.concatenate([small, moved]), jnp.concatenate([moved, small])
                )
            return small[None]

        for axis in ("c", "y", "x"):
            small = spread(small, axis)
        line_one = together(
            *[
                place(
                    [after(part, small)[:, cut] for part in around],
                    spots("z"),
                    (n_z, depth, wide),
                    0,
                )
                for cut in (slice(0, wide), slice(wide, 2 * wide))
            ]
        )
        shard_two = crossed(after(shards[1], around[1]))
        shard_three = crossed(after(shards[2], around[1]))

        small = spread(after(small, *line_one), "z")
        square_one = step_one(*line_one, small)

        def both_images(value):
            value = jnp.pad(value, ((0, ROWS - SEQ), (0, 0)))
            return jnp.concatenate([value, swap(value)])

        inputs = both_images(after(tokens, *square_one))
        down = both_images(after(cotangent, *square_one))
        line_two = lax.all_gather(shard_two, "z", axis=0)
        line_three = lax.all_gather(after(shard_three, *line_one), "z", axis=0)
        share = ln1_gain.shape[0]
        small = small.reshape(n_z, n_x, 2, 2, -1)
        small = small.transpose(0, 1, 3, 2, 4)
        vectors = small[..., : 6 * share].reshape(-1, 6, share).transpose(1, 0, 2).reshape(6, -1)
        vectors = jnp.pad(vectors.astype(F32), ((0, 2), (0, 0)))
        mine = pick(small[..., 6 * share :], 3, c).astype(F32)
        per_qv = qv_bias.shape[2]
        n_qv = qv_bias.size
        qv_half = mine[..., :n_qv].reshape((-1,) + qv_bias.shape)
        qv_half = qv_half.transpose(1, 2, 0, 3).reshape(2, -1)
        per_fc1 = fc1_bias.shape[1]
        fc1_half = mine[..., n_qv:].reshape((-1,) + fc1_bias.shape)
        fc1_half = fc1_half.transpose(1, 0, 2).reshape(-1)

        normed_one = norm_one(inputs, vectors)

        half_two = halves(line_two, normed_one, down)
        attn_w = step_two(*square_one, *half_two)
        projected, probs, mixed = [None] * 2, [None] * 2, [None] * 2

        def attend_half(colour, rows):
            cut = slice(colour * quarter, (colour + 1) * quarter)
            bias = jnp.concatenate(
                [qv_half[0, cut], jnp.zeros((quarter,), F32), qv_half[1, cut]]
            )
            projected[colour] = (dot(rows, attn_w[colour][:, :n_qkv]) + bias).astype(BF16)
            mixed[colour], probs[colour] = attend(projected[colour], heads)

        def back_product(lefts, weights):
            return (dot(lefts[0], weights[0], NT) + dot(lefts[1], weights[1], NT)).astype(BF16)

        def eight(row):
            return jnp.broadcast_to(row.reshape(1, -1), (8, row.size))

        attend_half(0, normed_one)
        fc1_half = after(fc1_half, mixed[0])
        half_three = halves(line_three, mixed[0], fc1_half)
        square_two = step_one(*half_two, *half_three)
        attend_half(1, after(normed_one, *square_two))
        square_three = step_one(*half_three, mixed[1])
        block = ((width, quarter), lambda i: (0, 3))
        low = rows_product(mixed, attn_w, block, False)
        moved = [swap(part) for part in low]
        residual, normed_two = norm_two(inputs, low, moved, vectors)
        fc1_w = step_two(*square_two, normed_two)
        hidden, slope = [], []
        for colour, weight in enumerate(fc1_w):
            bias = fc1_half[colour * hidden_half : (colour + 1) * hidden_half]
            pre = dot(after(normed_two, *fc1_w), weight) + bias
            cdf = 0.5 * (1.0 + lax.erf(pre * (1.0 / math.sqrt(2.0))))
            density = jnp.exp(-0.5 * pre * pre) * (1.0 / math.sqrt(2.0 * math.pi))
            hidden.append((pre * cdf).astype(BF16))
            slope.append((cdf + pre * density).astype(BF16))

        grad_fc2 = [weight_grad_kernel(down, h) for h in hidden]
        fc2_one, fc2_given = scatter_one(*grad_fc2)
        fc2_w = step_two(*square_three, *fc2_given)
        down_late = after(down, *fc2_w)
        hidden_grad, unit_sums = [], []
        for weight, unit_slope in zip(fc2_w, slope):
            grad, total = hidden_back(down_late, weight, unit_slope)
            hidden_grad.append(grad)
            unit_sums.append(total[0])
        low = rows_product(hidden_grad, fc1_w, fixed(width, hidden_half), False)
        moved = [swap(part) for part in low]
        fc2_two = scatter_two(fc2_one, low[0])
        normed_late = after(normed_two, fc2_two[0])
        grad_fc1 = [weight_grad(normed_late, g) for g in hidden_grad]
        fc1_one, fc1_given = scatter_one(*grad_fc1)
        moved = [after(part, *fc1_given) for part in moved]
        resid_grad, attn_grad, sums_two = norm_two_back(low, moved, residual, down, vectors)

        fc2_lines = lines(fc2_two, attn_grad)
        scat_fc2 = scatter_three(fc2_lines)
        back_a, sums_a = attend_back(
            after(projected[0], fc2_lines), probs[0], attn_grad, attn_w[0], heads
        )
        grads_a = attention_weight_grad(normed_one, back_a, attn_grad, mixed[0])
        a_one, a_given = scatter_one(*grads_a)
        fc1_two = scatter_two(fc1_one, *a_given)
        a_two = scatter_two(a_one, fc1_two[0])
        back_b, sums_b = attend_back(
            after(projected[1], fc1_two[0], a_two[0]), probs[1], attn_grad, attn_w[1], heads
        )
        fc1_lines = lines(fc1_two, back_b)
        scat_fc1 = scatter_three(fc1_lines)
        a_lines = lines(a_two, fc1_lines)
        grads_b = attention_weight_grad(
            after(normed_one, a_lines, scat_fc2), back_b, attn_grad, mixed[1]
        )
        b_one, b_given = scatter_one(*grads_b)
        block = ((width, n_qkv), lambda i: (0, 0))
        low_own, low_other = rows_product((after(back_a, *b_given), back_b), attn_w, block, True)
        b_two = scatter_two(b_one, low_own)
        b_lines = lines(b_two, scat_fc1)
        attn_lines = jnp.concatenate([a_lines, b_lines], axis=2)
        scat_attn = scatter_three(attn_lines)
        moved = [after(swap(part), attn_lines) for part in low_other]
        grad_tokens, sums_one = norm_one_back(low_own, moved, inputs, resid_grad, vectors)
        scat_fc1, scat_fc2, scat_attn = [
            send(part, transpose) for part in (scat_fc1, scat_fc2, scat_attn)
        ]
        scat_attn = scat_attn.astype(F32)

        hidden_late = [after(h, grad_tokens) for h in hidden]
        block = fixed(width, hidden_half)
        low_own, low_other = rows_product(hidden_late, fc2_w, block, True)
        moved = [swap(part) for part in low_other]
        output = layer_output(residual, low_own, moved, vectors)

        six = [sums_one[0], sums_one[1]] + [sums_two[n] for n in range(4)]
        grad_qv = [sums_a[0], sums_b[0]]
        grad_fc1_shift = jnp.concatenate(unit_sums)
        halves = [g[:quarter] for g in grad_qv] + [g[2 * quarter :] for g in grad_qv]
        sums = jnp.concatenate(six + halves + [grad_fc1_shift])[None]
        for axis in ("z", "x", "y"):
            moved = [send(sums, shift(axis, k)) for k in range(1, sizes[axis])]
            sums = functools.reduce(jnp.add, moved, sums)
        moved = swap(sums)[0]
        sums = sums[0]
        spot = ((z * n_x + x) * 2 + c) * 2 + y
        small_own = (sums[: 6 * width] + moved[: 6 * width]).reshape(6, -1, share)
        small_own = pick(small_own, 1, spot)
        half = jnp.where(owner, sums[6 * width :], moved[6 * width :])
        deep = (z * n_x + x) * 2 + c
        grad_qv = half[: 4 * quarter].reshape(2, qv_bias.shape[1], -1, per_qv)
        grad_qv = pick(grad_qv, 2, deep)
        grad_fc1_bias = pick(half[4 * quarter :].reshape(fc1_bias.shape[0], -1, per_fc1), 1, deep)

        def joined(index):
            at = index * quarter
            cuts = [scat_attn[:, at + half : at + half + quarter] for half in (0, 4 * quarter)]
            return jnp.concatenate(cuts, axis=1)

        grad_qkv = jnp.stack([joined(0), joined(1), joined(2)], axis=1)
        return (
            output,
            grad_tokens,
            small_own[0],
            small_own[1],
            grad_qkv,
            grad_qv,
            joined(3).T,
            small_own[4],
            small_own[2],
            small_own[3],
            scat_fc1.astype(F32),
            grad_fc1_bias,
            scat_fc2.astype(F32).T,
            small_own[5],
        )

    return on_device


def solution(mesh):
    chips = mesh.shape["dp"] // 2
    n_x = 1
    while n_x * n_x * 4 <= chips and chips % (n_x * 2) == 0:
        n_x *= 2
    n_z = chips // n_x
    fine = Mesh(np.asarray(mesh.devices).reshape(n_z, n_x, 2, 2), ALL)
    dp = ("z", "x", "c")
    every = P(ALL)
    rows = P(ALL, None)
    in_specs = (
        rows,
        every,
        every,
        P(dp, None, "y"),
        P(None, "y", dp),
        P("y", dp),
        every,
        every,
        every,
        P(dp, "y"),
        P("y", dp),
        P("y", dp),
        every,
        rows,
    )
    out_specs = (
        rows,
        rows,
        every,
        every,
        P(dp, None, "y"),
        P(None, "y", dp),
        P("y", dp),
        every,
        every,
        every,
        P(dp, "y"),
        P("y", dp),
        P("y", dp),
        every,
    )
    return jax.shard_map(
        build(n_z, n_x), mesh=fine, in_specs=in_specs, out_specs=out_specs, check_vma=False
    )
```

```python
import functools
import itertools
import math

import jax
import jax.numpy as jnp
import numpy as np
from jax import lax
from jax.experimental import pallas as pl
from jax.experimental.pallas import tpu as pltpu
from jax.experimental.layout import Layout, with_layout_constraint
from jax.sharding import Mesh
from jax.sharding import PartitionSpec as P

SEQ = 577
ROWS = 592
HEAD = 64
EPS = 1e-06
ALL = ("z", "x", "c", "y")
F32 = jnp.float32
BF16 = jnp.bfloat16

NN = (((1,), (0,)), ((), ()))
NT = (((1,), (1,)), ((), ()))
TN = (((0,), (0,)), ((), ()))
VMEM_LIMIT = 20 * 2**20
LITTLE = pl.CostEstimate(flops=2**20, bytes_accessed=2**18, transcendentals=0)


def rows_first(array):
    return with_layout_constraint(array, Layout(major_to_minor=(0, 1)))


def dot(left, right, dims=NN):
    return lax.dot_general(left, right, dims, preferred_element_type=F32)


def call(kernel, grid, ins, outs, *arrays):
    return pl.pallas_call(
        kernel,
        grid=grid,
        in_specs=[pl.BlockSpec(block, at) for block, at in ins],
        out_specs=[pl.BlockSpec(block, at) for block, at, _, _ in outs],
        out_shape=[jax.ShapeDtypeStruct(shape, dtype) for _, _, shape, dtype in outs],
        compiler_params=pltpu.CompilerParams(vmem_limit_bytes=VMEM_LIMIT),
        cost_estimate=LITTLE,
    )(*arrays)


def image(width):
    return (ROWS, width), lambda i: (i, 0)


def other_image(width):
    return (ROWS, width), lambda i: (1 - i, 0)


def fixed(*block):
    return block, lambda *i: (0,) * len(block)


def row_stats(values):
    mean = jnp.mean(values, axis=-1, keepdims=True)
    centered = values - mean
    inv = lax.rsqrt(jnp.mean(jnp.square(centered), axis=-1, keepdims=True) + EPS)
    return centered * inv, inv


def norm_back(upstream, normed, inv_scale, gain):
    scaled = upstream * gain
    first = jnp.mean(scaled, axis=-1, keepdims=True)
    second = jnp.mean(scaled * normed, axis=-1, keepdims=True)
    return inv_scale * (scaled - first - normed * second)


def norm_one(tokens, vectors):
    width = tokens.shape[1]

    def kernel(tokens_ref, vec_ref, out_ref):
        hat, _ = row_stats(tokens_ref[...].astype(F32))
        out_ref[...] = (hat * vec_ref[0:1] + vec_ref[1:2]).astype(BF16)

    out = image(width) + (tokens.shape, BF16)
    return call(kernel, (2,), [image(width), fixed(8, width)], [out], tokens, vectors)[0]


def attend(projected, heads):
    width = heads * HEAD

    def kernel(qkv_ref, mixed_ref, probs_ref):
        lane = lax.broadcasted_iota(jnp.int32, (ROWS, 128), 1)
        row = lax.broadcasted_iota(jnp.int32, (ROWS, ROWS), 0)
        for pair in range(heads // 2):
            at = pair * 128
            queries = qkv_ref[:, at : at + 128]
            keys = qkv_ref[:, width + at : width + at + 128]
            values = qkv_ref[:, 2 * width + at : 2 * width + at + 128]
            mixed = []
            for half in range(2):
                inside = (lane < HEAD) if half == 0 else (lane >= HEAD)
                own_keys = jnp.where(inside, keys, jnp.zeros_like(keys)) * BF16(0.125)
                scores = dot(own_keys, queries, NT)
                scores = jnp.where(row < SEQ, scores, -1e30)
                shifted = jnp.exp(scores - jnp.max(scores, axis=0, keepdims=True))
                total = jnp.sum(shifted, axis=0, keepdims=True)
                probs = (shifted * (1.0 / total)).astype(BF16)
                probs_ref[0, 2 * pair + half] = probs
                mixed.append(dot(probs, values, TN))
            mixed_ref[:, at : at + 128] = jnp.where(lane < HEAD, mixed[0], mixed[1]).astype(BF16)

    rows = 2 * ROWS
    return call(
        kernel,
        (2,),
        [image(3 * width)],
        [
            image(width) + ((rows, width), BF16),
            ((1, heads, ROWS, ROWS), lambda i: (i, 0, 0, 0), (2, heads, ROWS, ROWS), BF16),
        ],
        projected,
    )


def attend_back(projected, probs, attn_grad, weight, heads):
    width = heads * HEAD
    deep = attn_grad.shape[1]

    def kernel(qkv_ref, probs_ref, grad_ref, weight_ref, out_ref, sums_ref, mixed_ref):
        mixed_ref[...] = dot(grad_ref[...], weight_ref[...]).astype(BF16)
        lane = lax.broadcasted_iota(jnp.int32, (ROWS, 128), 1)
        for pair in range(heads // 2):
            at = pair * 128
            queries = qkv_ref[:, at : at + 128]
            keys = qkv_ref[:, width + at : width + at + 128]
            values = qkv_ref[:, 2 * width + at : 2 * width + at + 128]
            grad = mixed_ref[:, at : at + 128]
            keys_t = (keys * BF16(0.125)).T
            queries_s = queries * BF16(0.125)
            d_query, d_key, d_value = [], [], []
            for half in range(2):
                inside = (lane < HEAD) if half == 0 else (lane >= HEAD)
                own_values = jnp.where(inside, values, jnp.zeros_like(values))
                low_probs = probs_ref[0, 2 * pair + half]
                prob_grad = dot(own_values, grad, NT)
                wide_probs = low_probs.astype(F32)
                product = prob_grad * wide_probs
                weighted = jnp.sum(product, axis=0, keepdims=True)
                score_grad = (product - wide_probs * weighted).astype(BF16)
                d_value.append(dot(low_probs, grad))
                d_key.append(dot(score_grad, queries_s))
                d_query.append(dot(keys_t[half * HEAD : (half + 1) * HEAD], score_grad))
            parts = [
                jnp.concatenate(d_query, 0).T,
                jnp.where(lane < HEAD, d_key[0], d_key[1]),
                jnp.where(lane < HEAD, d_value[0], d_value[1]),
            ]
            for n, part in enumerate(parts):
                out_ref[:, n * width + at : n * width + at + 128] = part.astype(BF16)
        total = jnp.sum(out_ref[...].astype(F32), axis=0, keepdims=True)
        total = jnp.broadcast_to(total, sums_ref.shape)

        @pl.when(pl.program_id(0) == 0)
        def _():
            sums_ref[...] = total

        @pl.when(pl.program_id(0) != 0)
        def _():
            sums_ref[...] += total

    return pl.pallas_call(
        kernel,
        grid=(2,),
        in_specs=[
            pl.BlockSpec(*image(3 * width)),
            pl.BlockSpec((1, heads, ROWS, ROWS), lambda i: (i, 0, 0, 0)),
            pl.BlockSpec(*image(deep)),
            pl.BlockSpec((deep, width), lambda i: (0, 3)),
        ],
        out_specs=[pl.BlockSpec(*image(3 * width)), pl.BlockSpec(*fixed(8, 3 * width))],
        out_shape=[
            jax.ShapeDtypeStruct((2 * ROWS, 3 * width), BF16),
            jax.ShapeDtypeStruct((8, 3 * width), F32),
        ],
        scratch_shapes=[pltpu.VMEM((ROWS, width), BF16)],
        compiler_params=pltpu.CompilerParams(vmem_limit_bytes=VMEM_LIMIT),
        cost_estimate=LITTLE,
    )(projected, probs, attn_grad, weight)


def pieces(width):
    unit = width // 128
    part = -(-unit // 3) * 128
    return [part, part, width - 2 * part]


def joined_columns(refs):
    return jnp.concatenate([ref[...] for ref in refs], axis=1).astype(F32)


def rows_product(lefts, weights, block, split):
    width = lefts[0].shape[1]
    deep = weights[0].shape[0]
    count = len(lefts)
    cuts = pieces(deep)

    def kernel(*refs):
        outs = refs[2 * count :]
        total = dot(refs[0][...], refs[count][...], NT)
        for n in range(1, count):
            total = total + dot(refs[n][...], refs[count + n][...], NT)
        total = total.astype(BF16)

        def put(refs_out):
            at = 0
            for ref, cut in zip(refs_out, cuts):
                ref[...] = total[:, at : at + cut]
                at += cut

        if not split:
            put(outs)
            return

        @pl.when(pl.program_id(0) == 0)
        def _():
            outs[0][...] = total

        @pl.when(pl.program_id(0) != 0)
        def _():
            put(outs[1:])

    if split:
        outs = [fixed(ROWS, deep) + ((ROWS, deep), BF16)]
        outs += [fixed(ROWS, cut) + ((ROWS, cut), BF16) for cut in cuts]
    else:
        outs = [image(cut) + ((2 * ROWS, cut), BF16) for cut in cuts]
    ins = [image(width)] * count + [block] * count
    found = call(kernel, (2,), ins, outs, *lefts, *weights)
    return (found[0], found[1:]) if split else found


def norm_two(tokens, low, moved, vectors):
    width = tokens.shape[1]
    count = len(low)

    def kernel(tokens_ref, vec_ref, *refs):
        resid_ref, out_ref = refs[2 * count :]
        branch = joined_columns(refs[:count]) + joined_columns(refs[count : 2 * count])
        residual = tokens_ref[...].astype(F32) + branch + vec_ref[4:5]
        resid_ref[...] = residual
        hat, _ = row_stats(residual)
        out_ref[...] = (hat * vec_ref[2:3] + vec_ref[3:4]).astype(BF16)

    ins = [image(width), fixed(8, width)]
    ins += [image(part.shape[1]) for part in low] + [other_image(part.shape[1]) for part in moved]
    outs = [image(width) + (tokens.shape, F32), image(width) + (tokens.shape, BF16)]
    return call(kernel, (2,), ins, outs, tokens, vectors, *low, *moved)


def hidden_units(normed, weight, bias):
    deep, width = weight.shape
    cut = 512

    def kernel(rows_ref, weight_ref, bias_ref, hidden_ref, slope_ref):
        pre = dot(rows_ref[...], weight_ref[...]) + bias_ref[0:1]
        cdf = 0.5 * (1.0 + lax.erf(pre * (1.0 / math.sqrt(2.0))))
        density = jnp.exp(-0.5 * pre * pre) * (1.0 / math.sqrt(2.0 * math.pi))
        hidden_ref[...] = (pre * cdf).astype(BF16)
        slope_ref[...] = (cdf + pre * density).astype(BF16)

    out = ((ROWS, cut), lambda j, i: (i, j), (2 * ROWS, width), BF16)
    return call(
        kernel,
        (width // cut, 2),
        [
            ((ROWS, deep), lambda j, i: (i, 0)),
            ((deep, cut), lambda j, i: (0, j)),
            ((8, cut), lambda j, i: (0, j)),
        ],
        [out, out],
        normed,
        weight,
        bias,
    )


def hidden_back(down, weight, slope):
    deep, width = weight.shape
    cut = 1024

    def kernel(rows_ref, weight_ref, slope_ref, out_ref, sums_ref):
        grad = (dot(rows_ref[...], weight_ref[...]) * slope_ref[...].astype(F32)).astype(BF16)
        out_ref[...] = grad
        total = jnp.sum(grad.astype(F32), axis=0, keepdims=True)
        total = jnp.broadcast_to(total, sums_ref.shape)

        @pl.when(pl.program_id(1) == 0)
        def _():
            sums_ref[...] = total

        @pl.when(pl.program_id(1) != 0)
        def _():
            sums_ref[...] += total

    return call(
        kernel,
        (width // cut, 2),
        [
            ((ROWS, deep), lambda j, i: (i, 0)),
            ((deep, cut), lambda j, i: (0, j)),
            ((ROWS, cut), lambda j, i: (i, j)),
        ],
        [
            ((ROWS, cut), lambda j, i: (i, j), (2 * ROWS, width), BF16),
            ((8, cut), lambda j, i: (0, j), (8, width), F32),
        ],
        down,
        weight,
        slope,
    )


def weight_grad_kernel(rows, grad):
    deep, width = rows.shape[1], grad.shape[1]
    cut = 256

    def kernel(rows_ref, grad_ref, out_ref):
        out_ref[...] = dot(rows_ref[...], grad_ref[...], TN).astype(BF16)

    return call(
        kernel,
        (deep // cut,),
        [((2 * ROWS, cut), lambda j: (0, j)), fixed(2 * ROWS, width)],
        [((cut, width), lambda j: (j, 0), (deep, width), BF16)],
        rows,
        grad,
    )[0]


def weight_grad(rows, grad):
    return rows_first(dot(rows, grad, TN).astype(BF16))


def attention_weight_grad(normed, qkv_grad, attn_grad, mixed):
    deep, width = normed.shape[1], mixed.shape[1]
    cut = 256
    half = 2 * width

    def kernel(normed_ref, qkv_ref, grad_ref, mixed_ref, first_ref, second_ref):
        grad = dot(normed_ref[...], qkv_ref[...], TN).astype(BF16)
        first_ref[...] = grad[:, :half]
        second_ref[:, :width] = grad[:, half:]
        second_ref[:, width:] = dot(grad_ref[...], mixed_ref[...], TN).astype(BF16)

    column = ((2 * ROWS, cut), lambda j: (0, j))
    out = ((cut, half), lambda j: (j, 0), (deep, half), BF16)
    return call(
        kernel,
        (deep // cut,),
        [column, fixed(2 * ROWS, 3 * width), column, fixed(2 * ROWS, width)],
        [out, out],
        normed,
        qkv_grad,
        attn_grad,
        mixed,
    )


def norm_two_back(low, moved, residual, down, vectors):
    width = residual.shape[1]
    count = len(low)

    def kernel(resid_ref, down_ref, vec_ref, *refs):
        own_ref, out_ref, sums_ref = refs[2 * count :]
        back = joined_columns(refs[:count]) + joined_columns(refs[count : 2 * count])
        upstream = down_ref[...].astype(F32)
        hat, inv = row_stats(resid_ref[...])
        grad = upstream + norm_back(back, hat, inv, vec_ref[2:3])
        out_ref[...] = grad.astype(BF16)

        @pl.when(pl.program_id(0) == 0)
        def _():
            own_ref[...] = grad
            for n, part in enumerate((back * hat, back, grad, upstream)):
                sums_ref[n : n + 1] = jnp.sum(part, axis=0, keepdims=True)

    ins = [image(width), image(width), fixed(8, width)]
    ins += [image(part.shape[1]) for part in low] + [other_image(part.shape[1]) for part in moved]
    outs = [
        fixed(ROWS, width) + ((ROWS, width), F32),
        image(width) + ((2 * ROWS, width), BF16),
        fixed(8, width) + ((8, width), F32),
    ]
    return call(kernel, (2,), ins, outs, residual, down, vectors, *low, *moved)


def norm_one_back(low, moved, tokens, grad, vectors):
    width = low.shape[1]
    count = len(moved)

    def kernel(low_ref, tokens_ref, grad_ref, vec_ref, *refs):
        out_ref, sums_ref = refs[count:]
        back = low_ref[...].astype(F32) + joined_columns(refs[:count])
        hat, inv = row_stats(tokens_ref[...].astype(F32))
        total = grad_ref[...] + norm_back(back, hat, inv, vec_ref[0:1])
        out_ref[...] = total[:SEQ]
        for n, part in enumerate((back * hat, back)):
            sums_ref[n : n + 1] = jnp.sum(part, axis=0, keepdims=True)

    own_rows = fixed(ROWS, width)
    ins = [own_rows, own_rows, own_rows, fixed(8, width)]
    ins += [fixed(ROWS, part.shape[1]) for part in moved]
    outs = [fixed(SEQ, width) + ((SEQ, width), F32), fixed(8, width) + ((8, width), F32)]
    return call(kernel, (1,), ins, outs, low, tokens, grad, vectors, *moved)


def layer_output(residual, low, moved, vectors):
    width = low.shape[1]

    def kernel(resid_ref, low_ref, vec_ref, *refs):
        branch = low_ref[...].astype(F32) + joined_columns(refs[:-1])
        refs[-1][...] = (resid_ref[...] + branch + vec_ref[5:6]).astype(BF16)[:SEQ]

    own_rows = fixed(ROWS, width)
    out = fixed(SEQ, width) + ((SEQ, width), BF16)
    ins = [own_rows, own_rows, fixed(8, width)] + [fixed(ROWS, p.shape[1]) for p in moved]
    return call(kernel, (1,), ins, [out], residual, low, vectors, *moved)[0]


def place(parts, spots, shape, dim):
    part = parts[0].shape
    block = shape[:dim] + (1,) + shape[dim + 1 :]
    before, later = (0,) * dim, (0,) * (len(shape) - dim - 1)

    def kernel(spot_ref, *refs):
        out_ref = refs[-1]
        for n in range(len(parts)):

            @pl.when(pl.program_id(0) == n)
            def _():
                out_ref[...] = refs[n][...].reshape(block)

    return pl.pallas_call(
        kernel,
        grid_spec=pltpu.PrefetchScalarGridSpec(
            num_scalar_prefetch=1,
            grid=(len(parts),),
            in_specs=[pl.BlockSpec(part, lambda i, spot: (0,) * len(part))] * len(parts),
            out_specs=pl.BlockSpec(block, lambda i, spot: before + (spot[i],) + later),
        ),
        out_shape=jax.ShapeDtypeStruct(shape, parts[0].dtype),
        compiler_params=pltpu.CompilerParams(vmem_limit_bytes=VMEM_LIMIT),
        cost_estimate=LITTLE,
    )(spots, *parts)


def at_index(parts, index):
    found = parts[0]
    for n in range(1, len(parts)):
        found = jnp.where(index == n, parts[n], found)
    return found


def prefetched(kernel, spots, steps, ins, outs, arrays):
    return pl.pallas_call(
        kernel,
        grid_spec=pltpu.PrefetchScalarGridSpec(
            num_scalar_prefetch=1,
            grid=(steps,),
            in_specs=[pl.BlockSpec(block, at) for block, at in ins],
            out_specs=[pl.BlockSpec(block, at) for block, at, _ in outs],
        ),
        out_shape=[jax.ShapeDtypeStruct(shape, BF16) for _, _, shape in outs],
        compiler_params=pltpu.CompilerParams(vmem_limit_bytes=VMEM_LIMIT),
        cost_estimate=LITTLE,
    )(spots, *arrays)


def parts_to_give(first, second, spots, wide, columns):
    n_z, n_x, _, depth, _ = first.shape
    at_a, at_b = columns

    def kernel(spot_ref, *refs):
        half = len(refs) // 2
        for n in range(half):
            refs[half + n][...] = refs[n][...].reshape(refs[half + n].shape)

    ins = [((1, n_x, 1, depth, wide), lambda i, s: (i, 0, s[1], 0, at_a))]
    outs = [((1, n_x, depth, wide), lambda i, s: (i, 0, 0, 0), (n_z, n_x, depth, wide))]
    for k in range(1, n_x):
        ins.append(((1, 1, 2, depth, wide), lambda i, s, k=k: (i, s[2 + k], 0, 0, at_b)))
        outs.append(((1, 2, depth, wide), lambda i, s: (i, 0, 0, 0), (n_z, 2, depth, wide)))
    arrays = [first] + [second] * (n_x - 1)
    found = prefetched(kernel, spots, n_z, ins, outs, arrays)
    return found[0], found[1:]


def sums_to_give(first, first_moved, second, second_moved, spots, wide, columns):
    n_z, n_x, _, depth, _ = first.shape
    at_a, at_b = columns

    def kernel(spot_ref, first_ref, moved_ref, second_ref, *refs):
        moved_refs, outs = refs[: n_x - 1], refs[n_x - 1 :]
        sums = []
        for x in range(n_x):
            total = first_ref[0, x, 0].astype(F32) + moved_ref[0, x].astype(F32)
            sums.append(total)
        for k in range(n_x):
            outs[k][0] = at_index(sums, spot_ref[2 + k]).astype(BF16)
        sums = []
        for y in range(2):
            total = second_ref[0, 0, y].astype(F32)
            for ref in moved_refs:
                total = total + ref[0, y].astype(F32)
            sums.append(total)
        for k in range(2):
            outs[n_x + k][0] = at_index(sums, spot_ref[k]).astype(BF16)

    ins = [
        ((1, n_x, 1, depth, wide), lambda i, s: (i, 0, s[0], 0, at_a)),
        ((1, n_x, depth, wide), lambda i, s: (i, 0, 0, 0)),
        ((1, 1, 2, depth, wide), lambda i, s: (i, s[2], 0, 0, at_b)),
    ] + [((1, 2, depth, wide), lambda i, s: (i, 0, 0, 0))] * (n_x - 1)
    out = ((1, depth, wide), lambda i, s: (i, 0, 0), (n_z, depth, wide))
    arrays = [first, first_moved, second, *second_moved]
    found = prefetched(kernel, spots, n_z, ins, [out] * (n_x + 2), arrays)
    return found[0], found[1:n_x], found[n_x], found[n_x + 1]


def line_sums(first, first_moved, second, second_moved):
    n_z, depth, wide = first.shape

    def kernel(first_ref, *refs):
        count = len(first_moved)
        second_ref, moved_ref, out_ref = refs[count:]
        total = first_ref[0].astype(F32)
        for ref in refs[:count]:
            total = total + ref[0].astype(F32)
        out_ref[0, :, :wide] = total.astype(BF16)
        total = second_ref[0].astype(F32) + moved_ref[0].astype(F32)
        out_ref[0, :, wide:] = total.astype(BF16)

    block = ((1, depth, wide), lambda i: (i, 0, 0))
    out = ((1, depth, 2 * wide), lambda i: (i, 0, 0), (n_z, depth, 2 * wide), BF16)
    arrays = [first, *first_moved, second, second_moved]
    return call(kernel, (n_z,), [block] * len(arrays), [out], *arrays)[0]


def pack(qkv, proj, quarter):
    def kernel(qkv_ref, proj_ref, out_ref):
        for colour in range(2):
            cut = slice(colour * quarter, (colour + 1) * quarter)
            for n in range(4):
                at = (4 * colour + n) * quarter
                part = qkv_ref[n, :, cut] if n < 3 else proj_ref[:, cut]
                out_ref[:, at : at + quarter] = part

    return pl.pallas_call(
        kernel,
        out_shape=jax.ShapeDtypeStruct((proj.shape[0], 8 * quarter), proj.dtype),
        compiler_params=pltpu.CompilerParams(vmem_limit_bytes=VMEM_LIMIT),
        cost_estimate=LITTLE,
    )(qkv, proj)


def build(n_z, n_x):
    sizes = dict(z=n_z, x=n_x, c=2, y=2)

    def pairs(move, only=None):
        found = []
        names = ALL
        spots = list(itertools.product(*[range(sizes[a]) for a in names]))
        index = {spot: n for n, spot in enumerate(spots)}
        for spot in spots:
            here = dict(zip(names, spot))
            if only is not None and not only(here):
                continue
            there = dict(here)
            move(there)
            found.append((index[spot], index[tuple(there[a] for a in names)]))
        return found

    def shift(axis, by, only=None):
        def move(spot):
            spot[axis] = (spot[axis] + by) % sizes[axis]

        return pairs(move, only)

    def flip(axis, by):
        def move(spot):
            spot[axis] ^= by

        return pairs(move)

    def send(value, perm):
        return lax.ppermute(value, ALL, perm)

    def exchange(spot):
        spot["c"], spot["y"] = spot["y"], spot["c"]

    transpose = pairs(exchange)

    def on_device(
        tokens,
        ln1_gain,
        ln1_bias,
        qkv_weight,
        qv_bias,
        proj_weight,
        proj_bias,
        ln2_gain,
        ln2_bias,
        fc1_weight,
        fc1_bias,
        fc2_weight,
        fc2_bias,
        cotangent,
    ):
        z, x, c, y = [lax.axis_index(a) for a in ALL]
        owner = c == y
        where_am_i = dict(z=z, x=x, c=c, y=y)
        width = tokens.shape[1]
        depth = fc1_weight.shape[0]
        heads = qv_bias.shape[1] // 2

        def swap(value):
            return send(value, shift("c", 1))

        def after(value, *earlier):
            return lax.optimization_barrier((value,) + earlier)[0]

        quarter = proj_weight.shape[0] // 2
        n_qkv = 3 * quarter
        hidden_half = fc1_weight.shape[1] // 2
        proj_t = proj_weight.T
        fc2_t = fc2_weight.T
        shards = [pack(qkv_weight.transpose(1, 0, 2), proj_t, quarter), fc1_weight, fc2_t]

        def spots(axis):
            count = sizes[axis]
            return (where_am_i[axis] + jnp.arange(count, dtype=jnp.int32)) % count

        def from_all(value, axis, shape, dim, earlier=()):
            moved = [send(value, shift(axis, -k)) for k in range(1, sizes[axis])]
            if earlier:
                moved = [after(part, *earlier) for part in moved]
            return place([value] + moved, spots(axis), shape, dim)

        def crossed(shard):
            return send(shard, transpose)

        def together(*values):
            return lax.optimization_barrier(values)

        def halves(line, *earlier):
            wide = line.shape[2] // 2
            return together(line[:, :, :wide], line[:, :, wide:], *earlier)[:2]

        def step_one(first, second, *earlier):
            at = (n_z, n_x, depth, first.shape[2])
            first = from_all(first, "x", at, 1, earlier)
            at = (n_z, 2, depth, second.shape[2])
            second = from_all(second, "y", at, 1, earlier)
            return together(first, second)

        def step_two(first, second, *earlier):
            wide = first.shape[3]
            at = (n_z, n_x, 2, depth, wide)
            first = from_all(first, "y", at, 2, earlier)
            second = from_all(second, "x", at, 1, earlier)
            return first.reshape(width, wide), second.reshape(width, wide)

        def pick(array, axis, index):
            return lax.dynamic_index_in_dim(array, index, axis, keepdims=False)

        grad_spots = jnp.concatenate([spots("y"), spots("x")])

        def scatter_one(first, second, columns=(0, 0)):
            at = (n_z, n_x, 2, depth, first.shape[1])
            first, second = first.reshape(at), second.reshape(at)
            parts = first.shape[4] // (max(columns) + 1)
            to_y, to_x = parts_to_give(first, second, grad_spots, parts, columns)
            from_y = send(to_y, shift("y", 1))
            from_x = [send(part, shift("x", k + 1)) for k, part in enumerate(to_x)]
            return (first, from_y, second, from_x, parts, columns), (to_y, *to_x)

        def scatter_two(given, *earlier):
            first, from_y, second, from_x, parts, columns = given
            if earlier:
                from_y, from_x = after(from_y, *earlier), [after(v, *earlier) for v in from_x]
            own_a, to_x, own_b, to_y = sums_to_give(
                first, from_y, second, from_x, grad_spots, parts, columns
            )
            from_x = [send(part, shift("x", k + 1)) for k, part in enumerate(to_x)]
            return own_a, from_x, own_b, send(to_y, shift("y", 1))

        def lines(given, *earlier):
            own_a, from_x, own_b, from_y = given
            from_y, from_x = after(from_y, *earlier), [after(v, *earlier) for v in from_x]
            return line_sums(own_a, from_x, own_b, from_y)

        def scatter_three(both):
            return lax.psum_scatter(both, "z", scatter_dimension=0, tiled=False)

        shard_one = crossed(shards[0])
        wide = shards[0].shape[1] // 2
        around = [shard_one] + [send(shard_one, shift("z", -k)) for k in range(1, n_z)]

        small = jnp.concatenate(
            [after(ln1_gain, shard_one), ln1_bias, ln2_gain, ln2_bias, proj_bias, fc2_bias]
            + [qv_bias.reshape(-1), fc1_bias.reshape(-1)]
        )[None]

        def spread(small, axis):
            for n in range(sizes[axis].bit_length() - 1):
                moved = send(small, flip(axis, 2**n))
                low_side = (where_am_i[axis] // 2**n) % 2 == 0
                small = jnp.where(
                    low_side, jnp.concatenate([small, moved]), jnp.concatenate([moved, small])
                )
            return small[None]

        for axis in ("c", "y", "x"):
            small = spread(small, axis)
        line_one = together(
            *[
                place(
                    [after(part, small)[:, cut] for part in around],
                    spots("z"),
                    (n_z, depth, wide),
                    0,
                )
                for cut in (slice(0, wide), slice(wide, 2 * wide))
            ]
        )
        shard_two = crossed(after(shards[1], around[1]))
        shard_three = crossed(after(shards[2], around[1]))

        small = spread(after(small, *line_one), "z")
        square_one = step_one(*line_one, small)

        def both_images(value):
            value = jnp.pad(value, ((0, ROWS - SEQ), (0, 0)))
            return jnp.concatenate([value, swap(value)])

        inputs = both_images(after(tokens, around[1]))
        down = both_images(after(cotangent, around[1]))
        line_two = lax.all_gather(shard_two, "z", axis=0)
        line_three = lax.all_gather(after(shard_three, *line_one), "z", axis=0)
        share = ln1_gain.shape[0]
        small = small.reshape(n_z, n_x, 2, 2, -1)
        small = small.transpose(0, 1, 3, 2, 4)
        vectors = small[..., : 6 * share].reshape(-1, 6, share).transpose(1, 0, 2).reshape(6, -1)
        vectors = jnp.pad(vectors.astype(F32), ((0, 2), (0, 0)))
        mine = pick(small[..., 6 * share :], 3, c).astype(F32)
        per_qv = qv_bias.shape[2]
        n_qv = qv_bias.size
        qv_half = mine[..., :n_qv].reshape((-1,) + qv_bias.shape)
        qv_half = qv_half.transpose(1, 2, 0, 3).reshape(2, -1)
        per_fc1 = fc1_bias.shape[1]
        fc1_half = mine[..., n_qv:].reshape((-1,) + fc1_bias.shape)
        fc1_half = fc1_half.transpose(1, 0, 2).reshape(-1)

        normed_one = norm_one(inputs, vectors)

        half_two = halves(line_two, normed_one, down)
        attn_w = step_two(*square_one, *half_two)
        projected, probs, mixed = [None] * 2, [None] * 2, [None] * 2

        def attend_half(colour, rows):
            cut = slice(colour * quarter, (colour + 1) * quarter)
            bias = jnp.concatenate(
                [qv_half[0, cut], jnp.zeros((quarter,), F32), qv_half[1, cut]]
            )
            projected[colour] = (dot(rows, attn_w[colour][:, :n_qkv]) + bias).astype(BF16)
            mixed[colour], probs[colour] = attend(projected[colour], heads)

        def back_product(lefts, weights):
            return (dot(lefts[0], weights[0], NT) + dot(lefts[1], weights[1], NT)).astype(BF16)

        def eight(row):
            return jnp.broadcast_to(row.reshape(1, -1), (8, row.size))

        attend_half(0, normed_one)
        fc1_half = after(fc1_half, mixed[0])
        half_three = halves(line_three, mixed[0], fc1_half)
        square_two = step_one(*half_two, *half_three)
        attend_half(1, after(normed_one, *square_two))
        square_three = step_one(*half_three, mixed[1])
        block = ((width, quarter), lambda i: (0, 3))
        low = rows_product(mixed, attn_w, block, False)
        moved = [swap(part) for part in low]
        residual, normed_two = norm_two(inputs, low, moved, vectors)
        fc1_w = step_two(*square_two, normed_two)
        hidden, slope = [], []
        for colour, weight in enumerate(fc1_w):
            bias = fc1_half[colour * hidden_half : (colour + 1) * hidden_half]
            pre = dot(after(normed_two, *fc1_w), weight) + bias
            cdf = 0.5 * (1.0 + lax.erf(pre * (1.0 / math.sqrt(2.0))))
            density = jnp.exp(-0.5 * pre * pre) * (1.0 / math.sqrt(2.0 * math.pi))
            hidden.append((pre * cdf).astype(BF16))
            slope.append((cdf + pre * density).astype(BF16))

        grad_fc2 = [weight_grad_kernel(down, h) for h in hidden]
        fc2_one, fc2_given = scatter_one(*grad_fc2)
        fc2_w = step_two(*square_three, *fc2_given)
        down_late = after(down, *fc2_w)
        hidden_grad, unit_sums = [], []
        for weight, unit_slope in zip(fc2_w, slope):
            grad, total = hidden_back(down_late, weight, unit_slope)
            hidden_grad.append(grad)
            unit_sums.append(total[0])
        low = rows_product(hidden_grad, fc1_w, fixed(width, hidden_half), False)
        moved = [swap(part) for part in low]
        fc2_two = scatter_two(fc2_one, low[0])
        normed_late = after(normed_two, fc2_two[0])
        grad_fc1 = [weight_grad(normed_late, g) for g in hidden_grad]
        fc1_one, fc1_given = scatter_one(*grad_fc1)
        moved = [after(part, *fc1_given) for part in moved]
        resid_grad, attn_grad, sums_two = norm_two_back(low, moved, residual, down, vectors)

        fc2_lines = lines(fc2_two, attn_grad)
        scat_fc2 = scatter_three(fc2_lines)
        back_a, sums_a = attend_back(
            after(projected[0], fc2_lines), probs[0], attn_grad, attn_w[0], heads
        )
        grads_a = attention_weight_grad(normed_one, back_a, attn_grad, mixed[0])
        a_one, a_given = scatter_one(*grads_a)
        fc1_two = scatter_two(fc1_one, *a_given)
        a_two = scatter_two(a_one, fc1_two[0])
        back_b, sums_b = attend_back(
            after(projected[1], fc1_two[0], a_two[0]), probs[1], attn_grad, attn_w[1], heads
        )
        fc1_lines = lines(fc1_two, back_b)
        scat_fc1 = scatter_three(fc1_lines)
        a_lines = lines(a_two, fc1_lines)
        grads_b = attention_weight_grad(
            after(normed_one, a_lines, scat_fc2), back_b, attn_grad, mixed[1]
        )
        b_one, b_given = scatter_one(*grads_b)
        block = ((width, n_qkv), lambda i: (0, 0))
        low_own, low_other = rows_product((after(back_a, *b_given), back_b), attn_w, block, True)
        b_two = scatter_two(b_one, low_own)
        b_lines = lines(b_two, scat_fc1)
        attn_lines = jnp.concatenate([a_lines, b_lines], axis=2)
        scat_attn = scatter_three(attn_lines)
        moved = [after(swap(part), attn_lines) for part in low_other]
        grad_tokens, sums_one = norm_one_back(low_own, moved, inputs, resid_grad, vectors)
        scat_fc1, scat_fc2, scat_attn = [
            send(part, transpose) for part in (scat_fc1, scat_fc2, scat_attn)
        ]
        scat_attn = scat_attn.astype(F32)

        hidden_late = [after(h, grad_tokens) for h in hidden]
        block = fixed(width, hidden_half)
        low_own, low_other = rows_product(hidden_late, fc2_w, block, True)
        moved = [swap(part) for part in low_other]
        output = layer_output(residual, low_own, moved, vectors)

        six = [sums_one[0], sums_one[1]] + [sums_two[n] for n in range(4)]
        grad_qv = [sums_a[0], sums_b[0]]
        grad_fc1_shift = jnp.concatenate(unit_sums)
        halves = [g[:quarter] for g in grad_qv] + [g[2 * quarter :] for g in grad_qv]
        sums = jnp.concatenate(six + halves + [grad_fc1_shift])[None]
        for axis in ("z", "x", "y"):
            moved = [send(sums, shift(axis, k)) for k in range(1, sizes[axis])]
            sums = functools.reduce(jnp.add, moved, sums)
        moved = swap(sums)[0]
        sums = sums[0]
        spot = ((z * n_x + x) * 2 + c) * 2 + y
        small_own = (sums[: 6 * width] + moved[: 6 * width]).reshape(6, -1, share)
        small_own = pick(small_own, 1, spot)
        half = jnp.where(owner, sums[6 * width :], moved[6 * width :])
        deep = (z * n_x + x) * 2 + c
        grad_qv = half[: 4 * quarter].reshape(2, qv_bias.shape[1], -1, per_qv)
        grad_qv = pick(grad_qv, 2, deep)
        grad_fc1_bias = pick(half[4 * quarter :].reshape(fc1_bias.shape[0], -1, per_fc1), 1, deep)

        def joined(index):
            at = index * quarter
            cuts = [scat_attn[:, at + half : at + half + quarter] for half in (0, 4 * quarter)]
            return jnp.concatenate(cuts, axis=1)

        grad_qkv = jnp.stack([joined(0), joined(1), joined(2)], axis=1)
        return (
            output,
            grad_tokens,
            small_own[0],
            small_own[1],
            grad_qkv,
            grad_qv,
            joined(3).T,
            small_own[4],
            small_own[2],
            small_own[3],
            scat_fc1.astype(F32),
            grad_fc1_bias,
            scat_fc2.astype(F32).T,
            small_own[5],
        )

    return on_device


def solution(mesh):
    chips = mesh.shape["dp"] // 2
    n_x = 1
    while n_x * n_x * 4 <= chips and chips % (n_x * 2) == 0:
        n_x *= 2
    n_z = chips // n_x
    fine = Mesh(np.asarray(mesh.devices).reshape(n_z, n_x, 2, 2), ALL)
    dp = ("z", "x", "c")
    every = P(ALL)
    rows = P(ALL, None)
    in_specs = (
        rows,
        every,
        every,
        P(dp, None, "y"),
        P(None, "y", dp),
        P("y", dp),
        every,
        every,
        every,
        P(dp, "y"),
        P("y", dp),
        P("y", dp),
        every,
        rows,
    )
    out_specs = (
        rows,
        rows,
        every,
        every,
        P(dp, None, "y"),
        P(None, "y", dp),
        P("y", dp),
        every,
        every,
        every,
        P(dp, "y"),
        P("y", dp),
        P("y", dp),
        every,
    )
    return jax.shard_map(
        build(n_z, n_x), mesh=fine, in_specs=in_specs, out_specs=out_specs, check_vma=False
    )
```
